32 devices in a mesh: groups: 2 (over x), gx: 16 (over z, y, core).
Axes of the slice: x: 2, y: 2, z: 4, core: 2. Of those that a mesh axis runs over, the one named last changes fastest.
Arguments:
- lifted_field: bfloat16 [20, 128, 128, 512], P(None, ('groups', 'gx')), parts along dimension 1, may hold values from -6 to 6
- saturation_grad: bfloat16 [128, 128, 512], P(('groups', 'gx')), parts along dimension 0, may hold values from -6 to 6
- readout: float32 [20], replicated, may hold values from -3 to 3
- spectral_weight: bfloat16 [2, 20, 20, 24, 1152], P(None, None, None, None, 'gx'), may hold values from -3 to 3
- point_weight: bfloat16 [20, 20], replicated, may hold values from -1.25 to 1.25
- point_bias: float32 [20], replicated, may hold values from -3 to 3
Outputs:
- grad_field: bfloat16 [20, 128, 128, 512], P(None, ('groups', 'gx')), parts along dimension 1
- grad_spectral: float32 [4, 20, 20, 24, 1152], P('groups', None, None, None, 'gx'), parts along dimension 0
- grad_point: float32 [40, 20], P('groups'), parts along dimension 0
- grad_bias: float32 [40], P('groups'), parts along dimension 0
The draws below stay inside these ranges and needn't reach their ends.
There are 2 independent parts, one for each index of `groups`. The reference program is written for one: setup_inputs(seed, part) draws one part's arguments, and reference() takes and returns one part's arrays. A program takes and returns all parts, laid end to end along the dimension named above; an argument that names none is the same for every part. Nothing has to cross between parts.
All inputs are finite; a program needn't handle non-finite values.
Results may differ from the reference program's by a relative error of at most 0.02.
Values may be sent and summed in bfloat16 or wider, within the bound.
A program may use at most 256 MiB of HBM per device.

```python
import math
from functools import partial
import jax
import jax.numpy as jnp
from jax import lax

C = 20
NY = 128
NZ = 32
NT = 16
MX = 12
MY = 12
MZ = 6
MT = 4
NX = 64
NZT = 512
KZT = 48
MODES = 1152


def steps_of(rng, shape, pieces, low, high):
    level = 1.0
    for axis_at, blocks in pieces:
        draws = jax.random.uniform(jax.random.fold_in(jax.random.fold_in(rng, 6), axis_at), (blocks,), jnp.float32, low / len(pieces), high / len(pieces))
        level = level * jnp.repeat(jnp.exp(draws), shape[axis_at] // blocks).reshape((-1,) + (1,) * (len(shape) - 1 - axis_at))
    return level


def gaussian(key, shape, spread, bound, split=(), kind=jnp.bfloat16):
    loudness = steps_of(key, shape, split, -0.22, 0.18) if split else 1.0
    entries = jax.random.normal(key, shape, jnp.float32) * spread * loudness
    return jnp.minimum(jnp.maximum(entries, -bound), bound).astype(kind)


def setup_inputs(seed: int = 0, part: int = 0) -> dict:
    streams_of = jax.random.split(jax.random.key(seed), 7)
    part_keys = jax.random.split(jax.random.fold_in(streams_of[6], part), 7)
    return {
        "lifted_field": gaussian(part_keys[0], (C, NX, NY, NZT), 1.0, 6.0, ((1, 16),)),
        "saturation_grad": gaussian(part_keys[1], (NX, NY, NZT), 1.0, 6.0, ((0, 16),)),
        "readout": gaussian(streams_of[2], (C,), 1.0, 3.0, (), jnp.float32),
        "spectral_weight": gaussian(streams_of[3], (2, C, C, 2 * MX, MODES), 0.5, 3.0, ((4, 16),)),
        "point_weight": gaussian(streams_of[4], (C, C), C ** -0.5, 1.25),
        "point_bias": gaussian(streams_of[5], (C,), 0.5, 3.0, (), jnp.float32),
    }


def axis_tables(length, kept_modes):
    positions = jnp.arange(length, dtype=jnp.int32)
    frequency = jnp.concatenate([jnp.arange(kept_modes, dtype=jnp.int32), jnp.arange(length - kept_modes, length, dtype=jnp.int32)])
    phases = frequency[:, None] * positions[None, :] % length
    angles = phases.astype(jnp.float32) * (2.0 * math.pi / length)
    factor = 1.0 / math.sqrt(length)
    return (jnp.cos(angles) * factor, jnp.sin(angles) * factor)

def plane_tables():
    depth_cells = jnp.arange(NZ, dtype=jnp.int32)
    time_cells = jnp.arange(NT, dtype=jnp.int32)
    depth_freq = jnp.concatenate([jnp.arange(MZ, dtype=jnp.int32), jnp.arange(NZ - MZ, NZ, dtype=jnp.int32)])
    time_freq = jnp.arange(MT, dtype=jnp.int32)
    phases = (depth_freq[None, None, :, None] * depth_cells[:, None, None, None] * NT + time_freq[None, None, None, :] * time_cells[None, :, None, None] * NZ) % (NZ * NT)
    angles = phases.astype(jnp.float32) * (2.0 * math.pi / (NZ * NT))
    factor = 1.0 / math.sqrt(NZ * NT)
    cos_part = (jnp.cos(angles) * factor).reshape(NZ * NT, KZT)
    sin_part = (jnp.sin(angles) * factor).reshape(NZ * NT, KZT)
    doubling = jnp.where(time_freq == 0, 1.0, 2.0).astype(jnp.float32)
    weights = jnp.broadcast_to(doubling[None, :], (2 * MZ, MT)).reshape(KZT)
    forward_table = jnp.concatenate([cos_part, -sin_part], axis=1).astype(jnp.bfloat16)
    inverse_table = jnp.concatenate([(cos_part * weights[None, :]).T, (-sin_part * weights[None, :]).T], axis=0).astype(jnp.bfloat16)
    return (forward_table, inverse_table)

def widen(values):
    return lax.optimization_barrier(values.astype(jnp.bfloat16)).astype(jnp.float32)

def forward_pair(real_in, imag_in, cos_table, sin_table, pattern):
    apply = partial(jnp.einsum, pattern, precision=lax.Precision.HIGHEST)
    return (apply(cos_table, real_in) + apply(sin_table, imag_in), apply(cos_table, imag_in) - apply(sin_table, real_in))

def inverse_pair(real_in, imag_in, cos_table, sin_table, pattern):
    apply = partial(jnp.einsum, pattern, precision=lax.Precision.HIGHEST)
    return (apply(cos_table, real_in) - apply(sin_table, imag_in), apply(cos_table, imag_in) + apply(sin_table, real_in))

def lateral_forward(flat_field, lateral_cos, lateral_sin):
    channels, own_rows = (flat_field.shape[0], flat_field.shape[1])
    part_real, part_imag = forward_pair(flat_field[..., :KZT], flat_field[..., KZT:], lateral_cos, lateral_sin, 'ay,cxyk->cxak')
    return (part_real.reshape(channels, own_rows, MODES), part_imag.reshape(channels, own_rows, MODES))

def lateral_inverse(spec_real, spec_imag, lateral_cos, lateral_sin):
    channels, own_rows = (spec_real.shape[0], spec_real.shape[1])
    part_real = spec_real.reshape(channels, own_rows, 2 * MY, KZT)
    part_imag = spec_imag.reshape(channels, own_rows, 2 * MY, KZT)
    out_real, out_imag = inverse_pair(part_real, part_imag, lateral_cos, lateral_sin, 'ay,cxak->cxyk')
    return jnp.concatenate([out_real, out_imag], axis=-1)

def mode_mix(weight_real, weight_imag, spec_real, spec_imag):
    apply = partial(jnp.einsum, 'iokm,ikm->okm', precision=lax.Precision.HIGHEST)
    return (apply(weight_real, spec_real) - apply(weight_imag, spec_imag), apply(weight_real, spec_imag) + apply(weight_imag, spec_real))

def mode_adjoint(weight_real, weight_imag, spec_real, spec_imag, back_real, back_imag):
    outer = partial(jnp.einsum, 'ikm,okm->iokm', precision=lax.Precision.HIGHEST)
    grad_real = outer(spec_real, back_real) + outer(spec_imag, back_imag)
    grad_imag = outer(spec_real, back_imag) - outer(spec_imag, back_real)
    inner = partial(jnp.einsum, 'iokm,okm->ikm', precision=lax.Precision.HIGHEST)
    in_real = inner(weight_real, back_real) + inner(weight_imag, back_imag)
    in_imag = inner(weight_real, back_imag) - inner(weight_imag, back_real)
    return (jnp.stack([grad_real, grad_imag]), in_real, in_imag)

def gelu_slope(values):
    cumulative = 0.5 * (1.0 + jax.scipy.special.erf(values * 0.7071067811865476))
    density = jnp.exp(-0.5 * values * values) * 0.3989422804014327
    return cumulative + values * density

def reference(lifted_field, saturation_grad, readout, spectral_weight, point_weight, point_bias):
    highest = lax.Precision.HIGHEST
    forward_table, inverse_table = plane_tables()
    lateral_cos, lateral_sin = axis_tables(NY, MY)
    lateral_cos = widen(lateral_cos)
    lateral_sin = widen(lateral_sin)
    stream_cos, stream_sin = axis_tables(NX, MX)
    flat_field = jnp.dot(lifted_field.reshape(-1, NZT), forward_table, preferred_element_type=jnp.float32).reshape(C, NX, NY, 2 * KZT)
    spec_real, spec_imag = lateral_forward(widen(flat_field), lateral_cos, lateral_sin)
    spec_real, spec_imag = forward_pair(spec_real, spec_imag, stream_cos, stream_sin, 'ax,cxm->cam')
    weight_real = spectral_weight[0].astype(jnp.float32)
    weight_imag = spectral_weight[1].astype(jnp.float32)
    mixed_real, mixed_imag = mode_mix(weight_real, weight_imag, spec_real, spec_imag)
    back_real, back_imag = inverse_pair(mixed_real, mixed_imag, stream_cos, stream_sin, 'ax,cam->cxm')
    plane_back = lateral_inverse(widen(back_real), widen(back_imag), lateral_cos, lateral_sin).astype(jnp.bfloat16)
    spectral = jnp.dot(plane_back.reshape(-1, 2 * KZT), inverse_table, preferred_element_type=jnp.float32).reshape(lifted_field.shape)
    field_wide = lifted_field.astype(jnp.float32)
    point_term = jnp.einsum('io,ixyz->oxyz', point_weight.astype(jnp.float32), field_wide, precision=highest)
    pre_act = spectral + point_term + point_bias[:, None, None, None]
    upstream = readout[:, None, None, None] * saturation_grad.astype(jnp.float32)[None]
    grad_pre = (upstream * gelu_slope(pre_act)).astype(jnp.bfloat16)
    grad_wide = grad_pre.astype(jnp.float32)
    grad_point = jnp.einsum('ixyz,oxyz->io', field_wide, grad_wide, precision=highest)
    grad_bias = lax.optimization_barrier(jnp.sum(grad_wide, axis=(1, 2, 3)))
    flat_back = jnp.dot(grad_pre.reshape(-1, NZT), inverse_table.T, preferred_element_type=jnp.float32).reshape(C, NX, NY, 2 * KZT)
    adj_real, adj_imag = lateral_forward(widen(flat_back), lateral_cos, lateral_sin)
    adj_real, adj_imag = forward_pair(adj_real, adj_imag, stream_cos, stream_sin, 'ax,cxm->cam')
    grad_spectral, in_real, in_imag = mode_adjoint(weight_real, weight_imag, spec_real, spec_imag, adj_real, adj_imag)
    rows_real, rows_imag = inverse_pair(in_real, in_imag, stream_cos, stream_sin, 'ax,cam->cxm')
    plane_grad = lateral_inverse(widen(rows_real), widen(rows_imag), lateral_cos, lateral_sin).astype(jnp.bfloat16)
    spectral_in = jnp.dot(plane_grad.reshape(-1, 2 * KZT), forward_table.T, preferred_element_type=jnp.float32).reshape(lifted_field.shape)
    point_in = jnp.einsum('io,oxyz->ixyz', point_weight.astype(jnp.float32), grad_wide, precision=highest)
    grad_field = (spectral_in + point_in).astype(jnp.bfloat16)
    return (grad_field, grad_spectral, grad_point, grad_bias)
```

```python
from functools import partial
import math

import jax
import jax.numpy as jnp
import numpy as np
from jax import lax
from jax.experimental import pallas as pl
from jax.experimental.pallas import tpu as pltpu
from jax.sharding import PartitionSpec as P

NY = 128
NZ = 32
NT = 16
MX = 12
MY = 12
MZ = 6
MT = 4
NZT = 512
KZT = 48
KY = 2 * MY
KX = 2 * MX
LANES = 128
YB = 32
BF = jnp.bfloat16
F32 = jnp.float32
MESH = pl.DeviceIdType.MESH


def axis_tables(length, kept):
    positions = np.arange(length)
    frequency = np.concatenate([np.arange(kept), np.arange(length - kept, length)])
    angles = (frequency[:, None] * positions[None, :] % length) * (2.0 * math.pi / length)
    factor = 1.0 / math.sqrt(length)
    return np.cos(angles) * factor, np.sin(angles) * factor


def plane_tables():
    depth = np.concatenate([np.arange(MZ), np.arange(NZ - MZ, NZ)])
    phases = (
        depth[None, None, :, None] * np.arange(NZ)[:, None, None, None] * NT
        + np.arange(MT)[None, None, None, :] * np.arange(NT)[None, :, None, None] * NZ
    ) % NZT
    angles = phases * (2.0 * math.pi / NZT)
    factor = 1.0 / math.sqrt(NZT)
    cos_part = (np.cos(angles) * factor).reshape(NZT, KZT)
    sin_part = (np.sin(angles) * factor).reshape(NZT, KZT)
    weights = np.tile(np.where(np.arange(MT) == 0, 1.0, 2.0), 2 * MZ)
    forward = np.zeros((NZT, 2 * LANES))
    forward[:, :KZT], forward[:, LANES : LANES + KZT] = cos_part, -sin_part
    inverse = np.zeros((NZT, 2 * LANES))
    inverse[:, :KZT], inverse[:, LANES : LANES + KZT] = cos_part * weights, -sin_part * weights
    return forward, inverse


def narrow(table):
    return jnp.asarray(np.asarray(table, np.float32).astype(jnp.bfloat16))


def lateral_tables(rows):
    c, s = axis_tables(NY, MY)
    same = np.eye(rows)
    pairs = np.array([[c, s], [-s, c]])
    forward = np.einsum("rqky,xw->krxqwy", pairs, same)
    forward = forward.reshape(KY * 2 * rows, 2, rows, NY // YB, YB)
    forward = forward.transpose(3, 0, 1, 2, 4).reshape(NY // YB, KY * 2 * rows, 2 * rows * YB)
    inverse = np.einsum("rqky,xw->qwykrx", pairs, same)
    inverse = inverse.reshape(2, rows, NY // YB, YB, KY * 2 * rows)
    inverse = inverse.transpose(2, 0, 1, 3, 4).reshape(NY // YB, 2 * rows * YB, KY * 2 * rows)
    whole = np.einsum("rqky,xw->krxqwy", pairs, same).reshape(KY * 2 * rows, 2 * rows * NY)
    return narrow(forward), narrow(inverse), narrow(whole)


def stream_tables(cells, rows):
    c, s = axis_tables(cells, MX)
    pairs = np.array([[c, s], [-s, c]]).reshape(2, 2, KX, cells // rows, rows)
    table = np.einsum("rqkdx,ab->arkdbqx", pairs, np.eye(2))
    table = table.reshape(4 * KX, cells * 4)
    return narrow(table), narrow(table.T)


def mode_pieces(n):
    per = KY * KZT // n
    out = []
    for d in range(n):
        at, end, pieces = d * per, (d + 1) * per, []
        while at < end:
            ky, col = divmod(at, KZT)
            width = min(KZT - col, end - at)
            pieces.append((ky, col, width))
            at += width
        out.append(pieces)
    return out


def params(mib, **more):
    return pltpu.CompilerParams(vmem_limit_bytes=mib << 20, **more)


def dot(a, b):
    return jnp.dot(a, b, preferred_element_type=F32)


def pack(spectrum, out_ref, first_row, n, rr):
    for d, pieces in enumerate(mode_pieces(n)):
        halves = []
        for half in range(2):
            at = half * LANES
            parts = [
                spectrum[ky * rr : (ky + 1) * rr, at + col : at + col + width]
                for ky, col, width in pieces
            ]
            halves.append(jnp.concatenate(parts, axis=1))
        out_ref[d, pl.ds(first_row, 2 * rr), :] = jnp.concatenate(halves, axis=0).astype(BF)


def forward_kernel(n, rr, field_ref, plane_ref, lateral_ref, out_ref):
    cells = field_ref.shape[1] * NY
    flats = [
        dot(field_ref[half].reshape(cells, NZT), plane_ref[...]).astype(BF) for half in range(2)
    ]
    real = jnp.concatenate([f[:, :LANES] for f in flats], axis=1)
    imag = jnp.concatenate([f[:, LANES:] for f in flats], axis=1)
    spectrum = dot(lateral_ref[...], jnp.concatenate([real, imag], axis=0))
    pack(spectrum, out_ref, 0, n, rr)


def forward_call(field, plane_table, lateral_whole, n):
    channels, rows = field.shape[:2]
    rr = 2 * rows
    per = KY * KZT // n
    return pl.pallas_call(
        partial(forward_kernel, n, rr),
        grid=(channels // 2,),
        out_shape=jax.ShapeDtypeStruct((n, channels * rr, per), BF),
        in_specs=[
            pl.BlockSpec((2, rows, NY, NZT), lambda c: (c, 0, 0, 0)),
            pl.BlockSpec(plane_table.shape, lambda c: (0, 0)),
            pl.BlockSpec(lateral_whole.shape, lambda c: (0, 0)),
        ],
        out_specs=pl.BlockSpec((n, 2 * rr, per), lambda c: (0, c, 0)),
        compiler_params=params(40),
        name="forward",
    )(field, plane_table, lateral_whole)


def exchange(n, source, target, send, recv, local):
    me, group = lax.axis_index("gx"), lax.axis_index("groups")
    copies = []
    for k in range(1, n):
        peer = lax.rem(me + k, n)
        copy = pltpu.make_async_remote_copy(
            src_ref=source.at[peer],
            dst_ref=target.at[me],
            send_sem=send.at[k],
            recv_sem=recv.at[k],
            device_id=(group, peer),
            device_id_type=MESH,
        )
        copy.start()
        copies.append(copy)
    own = pltpu.make_async_copy(source.at[me], target.at[me], local)
    own.start()
    own.wait()
    return copies


def mix_kernel(
    n, rr, adjoint, sent, weight_hbm, stream_ref, back_ref, rows_out, spec_out,
    got, weights, mixed_wire, got_back, send, recv, local, weight_sem,
):
    channels = spec_out.shape[0]
    per = spec_out.shape[2]
    me, group = lax.axis_index("gx"), lax.axis_index("groups")
    barrier = pltpu.get_barrier_semaphore()
    for k in range(1, n):
        pl.semaphore_signal(
            barrier, inc=1, device_id=(group, lax.rem(me + k, n)), device_id_type=MESH
        )
    fetch = pltpu.make_async_copy(weight_hbm, weights, weight_sem)
    fetch.start()
    pl.semaphore_wait(barrier, n - 1)
    copies = exchange(n, sent, got, send.at[0], recv.at[0], local.at[0])
    for copy in copies:
        copy.wait()

    @pl.loop(0, channels // 2)
    def _(pair):
        block = got[:, pl.ds(pl.multiple_of(pair * 2 * rr, 16), 2 * rr), :]
        both = dot(stream_ref[...], block.reshape(n * 2 * rr, per))
        spec_out[2 * pair] = both[: 2 * KX]
        spec_out[2 * pair + 1] = both[2 * KX :]

    fetch.wait()

    @pl.loop(0, channels // 2)
    def _(pair):
        results = []
        for half in range(2):
            o = 2 * pair + half
            real = jnp.zeros((KX, per), F32)
            imag = jnp.zeros((KX, per), F32)
            for i in range(channels):
                at = (o, i) if adjoint else (i, o)
                w_real = weights[0, at[0], at[1]].astype(F32)
                w_imag = weights[1, at[0], at[1]].astype(F32)
                s_real = spec_out[i, :KX]
                s_imag = spec_out[i, KX:]
                if adjoint:
                    real += w_real * s_real + w_imag * s_imag
                    imag += w_real * s_imag - w_imag * s_real
                else:
                    real += w_real * s_real - w_imag * s_imag
                    imag += w_real * s_imag + w_imag * s_real
            results += [real, imag]
        both = dot(back_ref[...], jnp.concatenate(results, axis=0).astype(BF)).astype(BF)
        mixed_wire[:, pl.ds(pl.multiple_of(pair * 2 * rr, 16), 2 * rr), :] = both.reshape(
            n, 2 * rr, per
        )

    copies = exchange(n, mixed_wire, got_back, send.at[1], recv.at[1], local.at[1])
    for copy in copies:
        copy.wait()

    pieces_of = mode_pieces(n)

    @pl.loop(0, channels // 2)
    def _(pair):
        found = [[[] for _ in range(KY)] for _ in range(2)]
        for d in range(n):
            block = got_back[d, pl.ds(pl.multiple_of(pair * 2 * rr, 16), 2 * rr), :].astype(F32)
            at = 0
            for ky, _, width in pieces_of[d]:
                for half in range(2):
                    found[half][ky].append(block[half * rr : (half + 1) * rr, at : at + width])
                at += width
        lanes = jnp.zeros((rr, LANES - KZT), F32)
        halves = [
            jnp.concatenate(
                [jnp.concatenate(found[half][ky] + [lanes], axis=1) for ky in range(KY)], axis=0
            )
            for half in range(2)
        ]
        rows_out[pair] = jnp.concatenate(halves, axis=1).astype(BF)


def mix_call(sent, weight, stream, stream_back, n, adjoint):
    channels = weight.shape[1]
    rr = sent.shape[1] // channels
    per = sent.shape[2]
    return pl.pallas_call(
        partial(mix_kernel, n, rr, adjoint),
        out_shape=(
            jax.ShapeDtypeStruct((channels // 2, KY * rr, 2 * LANES), BF),
            jax.ShapeDtypeStruct((channels, 2 * KX, per), F32),
        ),
        in_specs=[
            pl.BlockSpec(memory_space=pltpu.VMEM),
            pl.BlockSpec(memory_space=pl.ANY),
            pl.BlockSpec(memory_space=pltpu.VMEM),
            pl.BlockSpec(memory_space=pltpu.VMEM),
        ],
        out_specs=(
            pl.BlockSpec(memory_space=pltpu.VMEM),
            pl.BlockSpec(memory_space=pltpu.VMEM),
        ),
        scratch_shapes=[
            pltpu.VMEM(sent.shape, BF),
            pltpu.VMEM(weight.shape, BF),
            pltpu.VMEM(sent.shape, BF),
            pltpu.VMEM(sent.shape, BF),
            pltpu.SemaphoreType.DMA((2, n)),
            pltpu.SemaphoreType.DMA((2, n)),
            pltpu.SemaphoreType.DMA((2,)),
            pltpu.SemaphoreType.DMA(()),
        ],
        compiler_params=params(40, collective_id=int(adjoint), has_side_effects=True),
        name="adjoint_mix" if adjoint else "mix",
    )(sent, weight, stream, stream_back)


def gelu_slope(v):
    a = jnp.abs(v)
    t = 1.0 / (1.0 + (0.3275911 * 0.7071067811865476) * a)
    e = jnp.exp(-0.5 * v * v)
    poly = 0.5 * 1.061405429
    for coefficient in (-1.453152027, 1.421413741, -0.284496736, 0.254829592):
        poly = poly * t + 0.5 * coefficient
    tail = e * (poly * t - 0.3989422804014327 * a)
    return jnp.where(v >= 0, 1.0 - tail, tail)


def planes(rows_ref, lateral, table, store, channels, cells):
    @pl.loop(0, channels // 2)
    def _(pair):
        flat = dot(lateral, rows_ref[pair]).astype(BF)
        for half in range(2):
            at = slice(half * LANES, (half + 1) * LANES)
            plane = jnp.concatenate([flat[:cells, at], flat[cells:, at]], axis=1)
            store(2 * pair + half, dot(plane, table))


def middle_kernel(
    n, rr, rows_ref, field_ref, sat_ref, readout_ref, bias_ref, kron_ref, inverse_ref, back_ref,
    lat_inv_ref, lat_fwd_ref, grad_ref, wire_ref, corr_ref, spectral, spectrum,
):
    step = pl.program_id(0)
    channels, rows = field_ref.shape[:2]
    cells = rows * YB

    @pl.when(step == 0)
    def _():
        corr_ref[...] = jnp.zeros_like(corr_ref)
        spectrum[...] = jnp.zeros_like(spectrum)

    def keep(o, value):
        spectral[o] = value.reshape(rows, YB, NZT)

    planes(rows_ref, lat_inv_ref[0], inverse_ref[...], keep, channels, cells)

    @pl.loop(0, rows)
    def _(x):
        @pl.loop(0, YB // 8)
        def _(yb):
            y8 = pl.ds(pl.multiple_of(yb * 8, 8), 8)
            block = field_ref[:, x, y8, :].reshape(channels * 8, NZT)
            point = dot(kron_ref[...], block)
            bias = jnp.concatenate([bias_ref[...]] * (NZT // LANES), axis=1)
            readout = jnp.concatenate([readout_ref[...]] * (NZT // LANES), axis=1)
            pre = point + spectral[:, x, y8, :].reshape(channels * 8, NZT) + bias
            sat = sat_ref[x, y8, :].astype(F32)
            up = readout * jnp.broadcast_to(sat[None], (channels, 8, NZT)).reshape(-1, NZT)
            grad = (up * gelu_slope(pre)).astype(BF)
            grad_ref[:, x, y8, :] = grad.reshape(channels, 8, NZT)
            left = jnp.concatenate([block, jnp.ones((16, NZT), BF)], axis=0)
            corr_ref[...] += lax.dot_general(
                left, grad, (((1,), (1,)), ((), ())), preferred_element_type=F32
            )

    @pl.loop(0, channels // 2)
    def _(pair):
        flats = [
            dot(grad_ref[2 * pair + half].reshape(cells, NZT), back_ref[...]).astype(BF)
            for half in range(2)
        ]
        real = jnp.concatenate([f[:, :LANES] for f in flats], axis=1)
        imag = jnp.concatenate([f[:, LANES:] for f in flats], axis=1)
        spectrum[pair] += dot(lat_fwd_ref[0], jnp.concatenate([real, imag], axis=0))

    @pl.when(step == pl.num_programs(0) - 1)
    def _():
        @pl.loop(0, channels // 2)
        def _(pair):
            pack(spectrum[pair], wire_ref, pl.multiple_of(pair * 2 * rr, 16), n, rr)


def middle_call(rows_in, field, sat, readout, bias, kron, inverse, back, lat_inv, lat_fwd, n):
    channels, rows = field.shape[:2]
    rr = 2 * rows
    per = KY * KZT // n
    whole = lambda a: pl.BlockSpec(a.shape, lambda y: (0,) * a.ndim)
    return pl.pallas_call(
        partial(middle_kernel, n, rr),
        grid=(NY // YB,),
        out_shape=(
            jax.ShapeDtypeStruct(field.shape, BF),
            jax.ShapeDtypeStruct((n, channels * rr, per), BF),
            jax.ShapeDtypeStruct((channels * 8 + 16, channels * 8), F32),
        ),
        in_specs=[
            whole(rows_in),
            pl.BlockSpec((channels, rows, YB, NZT), lambda y: (0, 0, y, 0)),
            pl.BlockSpec((rows, YB, NZT), lambda y: (0, y, 0)),
            whole(readout), whole(bias), whole(kron), whole(inverse), whole(back),
            pl.BlockSpec((1,) + lat_inv.shape[1:], lambda y: (y, 0, 0)),
            pl.BlockSpec((1,) + lat_fwd.shape[1:], lambda y: (y, 0, 0)),
        ],
        out_specs=(
            pl.BlockSpec((channels, rows, YB, NZT), lambda y: (0, 0, y, 0)),
            pl.BlockSpec((n, channels * rr, per), lambda y: (0, 0, 0)),
            pl.BlockSpec((channels * 8 + 16, channels * 8), lambda y: (0, 0)),
        ),
        scratch_shapes=[
            pltpu.VMEM((channels, rows, YB, NZT), F32),
            pltpu.VMEM((channels // 2, KY * rr, 2 * LANES), F32),
        ],
        compiler_params=params(48),
        name="middle",
    )(rows_in, field, sat, readout, bias, kron, inverse, back, lat_inv, lat_fwd)


def last_kernel(rows_ref, grad_ref, kron_ref, table_ref, lat_inv_ref, out_ref, spectral):
    channels, rows = grad_ref.shape[:2]
    cells = rows * YB

    def keep(o, value):
        spectral[o] = value.reshape(rows, YB, NZT)

    planes(rows_ref, lat_inv_ref[0], table_ref[...], keep, channels, cells)

    @pl.loop(0, rows)
    def _(x):
        @pl.loop(0, YB // 8)
        def _(yb):
            y8 = pl.ds(pl.multiple_of(yb * 8, 8), 8)
            block = grad_ref[:, x, y8, :].reshape(channels * 8, NZT)
            total = dot(kron_ref[...], block) + spectral[:, x, y8, :].reshape(channels * 8, NZT)
            out_ref[:, x, y8, :] = total.astype(BF).reshape(channels, 8, NZT)


def last_call(rows_in, grad, kron, table, lat_inv):
    channels, rows = grad.shape[:2]
    whole = lambda a: pl.BlockSpec(a.shape, lambda y: (0,) * a.ndim)
    block = pl.BlockSpec((channels, rows, YB, NZT), lambda y: (0, 0, y, 0))
    return pl.pallas_call(
        last_kernel,
        grid=(NY // YB,),
        out_shape=jax.ShapeDtypeStruct(grad.shape, BF),
        in_specs=[
            whole(rows_in), block, whole(kron), whole(table),
            pl.BlockSpec((1,) + lat_inv.shape[1:], lambda y: (y, 0, 0)),
        ],
        out_specs=block,
        scratch_shapes=[pltpu.VMEM((channels, rows, YB, NZT), F32)],
        compiler_params=params(48),
        name="last",
    )(rows_in, grad, kron, table, lat_inv)


def outer_kernel(spec_ref, back_ref, out_ref):
    s_real, s_imag = spec_ref[0, :KX], spec_ref[0, KX:]
    for o in range(back_ref.shape[0]):
        b_real, b_imag = back_ref[o, :KX], back_ref[o, KX:]
        out_ref[0, 0, o] = s_real * b_real + s_imag * b_imag
        out_ref[1, 0, o] = s_real * b_imag - s_imag * b_real


def outer_call(spec, back):
    channels, _, per = spec.shape
    return pl.pallas_call(
        outer_kernel,
        grid=(channels,),
        out_shape=jax.ShapeDtypeStruct((2, channels, channels, KX, per), F32),
        in_specs=[
            pl.BlockSpec((1, 2 * KX, per), lambda i: (i, 0, 0)),
            pl.BlockSpec(back.shape, lambda i: (0, 0, 0)),
        ],
        out_specs=pl.BlockSpec((2, 1, channels, KX, per), lambda i: (0, i, 0, 0, 0)),
        compiler_params=params(24),
        name="outer",
    )(spec, back)


def local(n, lifted_field, saturation_grad, readout, spectral_weight, point_weight, point_bias):
    channels, rows = lifted_field.shape[:2]
    forward_table, inverse_table = plane_tables()
    lat_fwd, lat_inv, lat_whole = lateral_tables(rows)
    stream, stream_back = stream_tables(rows * n, rows)
    eye = jnp.eye(8, dtype=BF)
    kron = jnp.kron(point_weight, eye)
    spread = lambda a: jnp.broadcast_to(jnp.repeat(a, 8)[:, None], (channels * 8, LANES))

    sent = forward_call(lifted_field, narrow(forward_table), lat_whole, n)
    rows_in, spec = mix_call(sent, spectral_weight, stream, stream_back, n, False)
    grad_pre, sent_back, corr = middle_call(
        rows_in, lifted_field, saturation_grad, spread(readout), spread(point_bias), kron.T,
        narrow(inverse_table.T), narrow(inverse_table), lat_inv, lat_fwd, n,
    )
    diagonal = jnp.einsum("iaoa->io", corr[: channels * 8].reshape(channels, 8, channels, 8))
    bias_part = corr[channels * 8].reshape(channels, 8).sum(axis=1)
    grad_point, grad_bias = lax.psum((diagonal, bias_part), "gx")
    rows_back, back_spec = mix_call(sent_back, spectral_weight, stream, stream_back, n, True)
    grad_spectral = outer_call(spec, back_spec)
    grad_field = last_call(rows_back, grad_pre, kron, narrow(forward_table.T), lat_inv)
    return (grad_field, grad_spectral, grad_point, grad_bias)


def solution(mesh):
    placed = (
        P(None, ("groups", "gx"), None, None),
        P(("groups", "gx"), None, None),
        P(),
        P(None, None, None, None, "gx"),
        P(),
        P(),
    )
    return jax.shard_map(
        partial(local, mesh.shape["gx"]),
        mesh=mesh,
        in_specs=placed,
        out_specs=(
            P(None, ("groups", "gx"), None, None),
            P("groups", None, None, None, "gx"),
            P("groups", None),
            P("groups"),
        ),
        check_vma=False,
    )
```

```python
from functools import partial
import math

import jax
import jax.numpy as jnp
import numpy as np
from jax import lax
from jax.experimental import pallas as pl
from jax.experimental.pallas import tpu as pltpu
from jax.sharding import PartitionSpec as P

NY = 128
NZ = 32
NT = 16
MX = 12
MY = 12
MZ = 6
MT = 4
NZT = 512
KZT = 48
KY = 2 * MY
KX = 2 * MX
LANES = 128
YB = 32
BF = jnp.bfloat16
F32 = jnp.float32
MESH = pl.DeviceIdType.MESH


def axis_tables(length, kept):
    positions = np.arange(length)
    frequency = np.concatenate([np.arange(kept), np.arange(length - kept, length)])
    angles = (frequency[:, None] * positions[None, :] % length) * (2.0 * math.pi / length)
    factor = 1.0 / math.sqrt(length)
    return np.cos(angles) * factor, np.sin(angles) * factor


def plane_tables():
    depth = np.concatenate([np.arange(MZ), np.arange(NZ - MZ, NZ)])
    phases = (
        depth[None, None, :, None] * np.arange(NZ)[:, None, None, None] * NT
        + np.arange(MT)[None, None, None, :] * np.arange(NT)[None, :, None, None] * NZ
    ) % NZT
    angles = phases * (2.0 * math.pi / NZT)
    factor = 1.0 / math.sqrt(NZT)
    cos_part = (np.cos(angles) * factor).reshape(NZT, KZT)
    sin_part = (np.sin(angles) * factor).reshape(NZT, KZT)
    weights = np.tile(np.where(np.arange(MT) == 0, 1.0, 2.0), 2 * MZ)
    forward = np.zeros((NZT, 2 * LANES))
    forward[:, :KZT], forward[:, LANES : LANES + KZT] = cos_part, -sin_part
    inverse = np.zeros((NZT, 2 * LANES))
    inverse[:, :KZT], inverse[:, LANES : LANES + KZT] = cos_part * weights, -sin_part * weights
    return forward, inverse


def narrow(table):
    return jnp.asarray(np.asarray(table, np.float32).astype(jnp.bfloat16))


def lateral_tables(rows):
    c, s = axis_tables(NY, MY)
    same = np.eye(rows)
    pairs = np.array([[c, s], [-s, c]])
    forward = np.einsum("rqky,xw->krxqwy", pairs, same)
    forward = forward.reshape(KY * 2 * rows, 2, rows, NY // YB, YB)
    forward = forward.transpose(3, 0, 1, 2, 4).reshape(NY // YB, KY * 2 * rows, 2 * rows * YB)
    inverse = np.einsum("rqky,xw->qwykrx", pairs, same)
    inverse = inverse.reshape(2, rows, NY // YB, YB, KY * 2 * rows)
    inverse = inverse.transpose(2, 0, 1, 3, 4).reshape(NY // YB, 2 * rows * YB, KY * 2 * rows)
    whole = np.einsum("rqky,xw->krxqwy", pairs, same).reshape(KY * 2 * rows, 2 * rows * NY)
    return narrow(forward), narrow(inverse), narrow(whole)


def stream_tables(cells, rows):
    c, s = axis_tables(cells, MX)
    pairs = np.array([[c, s], [-s, c]]).reshape(2, 2, KX, cells // rows, rows)
    table = np.einsum("rqkdx,ab->arkdbqx", pairs, np.eye(2))
    table = table.reshape(4 * KX, cells * 4)
    return narrow(table), narrow(table.T)


def mode_pieces(n):
    per = KY * KZT // n
    out = []
    for d in range(n):
        at, end, pieces = d * per, (d + 1) * per, []
        while at < end:
            ky, col = divmod(at, KZT)
            width = min(KZT - col, end - at)
            pieces.append((ky, col, width))
            at += width
        out.append(pieces)
    return out


def params(mib, **more):
    return pltpu.CompilerParams(vmem_limit_bytes=mib << 20, **more)


def dot(a, b):
    return jnp.dot(a, b, preferred_element_type=F32)


def pack(spectrum, out_ref, first_row, n, rr):
    for d, pieces in enumerate(mode_pieces(n)):
        halves = []
        for half in range(2):
            at = half * LANES
            parts = [
                spectrum[ky * rr : (ky + 1) * rr, at + col : at + col + width]
                for ky, col, width in pieces
            ]
            halves.append(jnp.concatenate(parts, axis=1))
        out_ref[d, pl.ds(first_row, 2 * rr), :] = jnp.concatenate(halves, axis=0).astype(BF)


def forward_kernel(n, rr, field_ref, plane_ref, lateral_ref, out_ref):
    cells = field_ref.shape[1] * NY
    flats = [
        dot(field_ref[half].reshape(cells, NZT), plane_ref[...]).astype(BF) for half in range(2)
    ]
    real = jnp.concatenate([f[:, :LANES] for f in flats], axis=1)
    imag = jnp.concatenate([f[:, LANES:] for f in flats], axis=1)
    spectrum = dot(lateral_ref[...], jnp.concatenate([real, imag], axis=0))
    pack(spectrum, out_ref, 0, n, rr)


def forward_call(field, plane_table, lateral_whole, n):
    channels, rows = field.shape[:2]
    rr = 2 * rows
    per = KY * KZT // n
    return pl.pallas_call(
        partial(forward_kernel, n, rr),
        grid=(channels // 2,),
        out_shape=jax.ShapeDtypeStruct((n, channels * rr, per), BF),
        in_specs=[
            pl.BlockSpec((2, rows, NY, NZT), lambda c: (c, 0, 0, 0)),
            pl.BlockSpec(plane_table.shape, lambda c: (0, 0)),
            pl.BlockSpec(lateral_whole.shape, lambda c: (0, 0)),
        ],
        out_specs=pl.BlockSpec((n, 2 * rr, per), lambda c: (0, c, 0)),
        compiler_params=params(60),
        name="forward",
    )(field, plane_table, lateral_whole)


def exchange(n, source, target, send, recv, local):
    me, group = lax.axis_index("gx"), lax.axis_index("groups")
    copies = []
    for k in range(1, n):
        peer = lax.rem(me + k, n)
        copy = pltpu.make_async_remote_copy(
            src_ref=source.at[peer],
            dst_ref=target.at[me],
            send_sem=send.at[k],
            recv_sem=recv.at[k],
            device_id=(group, peer),
            device_id_type=MESH,
        )
        copy.start()
        copies.append(copy)
    own = pltpu.make_async_copy(source.at[me], target.at[me], local)
    own.start()
    own.wait()
    return copies


def spread_parts(n, source, target, send, recv, local):
    me, group = lax.axis_index("gx"), lax.axis_index("groups")
    copies = []
    for k in range(1, n):
        copy = pltpu.make_async_remote_copy(
            src_ref=source,
            dst_ref=target.at[me],
            send_sem=send.at[k],
            recv_sem=recv.at[k],
            device_id=(group, lax.rem(me + k, n)),
            device_id_type=MESH,
        )
        copy.start()
        copies.append(copy)
    own = pltpu.make_async_copy(source, target.at[me], local)
    own.start()
    own.wait()
    return copies


def mix_kernel(
    n, rr, adjoint, sent, weight_hbm, stream_ref, back_ref, *refs
):
    if adjoint:
        part_ref, rows_out, spec_out, total_ref, *refs = refs
        *refs, parts, part_send, part_recv, part_local = refs
    else:
        rows_out, spec_out, *refs = refs
    got, weights, mixed_wire, got_back, send, recv, local, weight_sem = refs
    channels = spec_out.shape[0]
    per = spec_out.shape[2]
    me, group = lax.axis_index("gx"), lax.axis_index("groups")
    barrier = pltpu.get_barrier_semaphore()
    for k in range(1, n):
        pl.semaphore_signal(
            barrier, inc=1, device_id=(group, lax.rem(me + k, n)), device_id_type=MESH
        )
    fetch = pltpu.make_async_copy(weight_hbm, weights, weight_sem)
    fetch.start()
    pl.semaphore_wait(barrier, n - 1)
    copies = exchange(n, sent, got, send.at[0], recv.at[0], local.at[0])
    for copy in copies:
        copy.wait()

    @pl.loop(0, channels // 2)
    def _(pair):
        block = got[:, pl.ds(pl.multiple_of(pair * 2 * rr, 16), 2 * rr), :]
        both = dot(stream_ref[...], block.reshape(n * 2 * rr, per))
        spec_out[2 * pair] = both[: 2 * KX]
        spec_out[2 * pair + 1] = both[2 * KX :]

    fetch.wait()

    @pl.loop(0, channels // 2)
    def _(pair):
        results = []
        for half in range(2):
            o = 2 * pair + half
            real = jnp.zeros((KX, per), F32)
            imag = jnp.zeros((KX, per), F32)
            for i in range(channels):
                at = (o, i) if adjoint else (i, o)
                w_real = weights[0, at[0], at[1]].astype(F32)
                w_imag = weights[1, at[0], at[1]].astype(F32)
                s_real = spec_out[i, :KX]
                s_imag = spec_out[i, KX:]
                if adjoint:
                    real += w_real * s_real + w_imag * s_imag
                    imag += w_real * s_imag - w_imag * s_real
                else:
                    real += w_real * s_real - w_imag * s_imag
                    imag += w_real * s_imag + w_imag * s_real
            results += [real, imag]
        both = dot(back_ref[...], jnp.concatenate(results, axis=0).astype(BF)).astype(BF)
        mixed_wire[:, pl.ds(pl.multiple_of(pair * 2 * rr, 16), 2 * rr), :] = both.reshape(
            n, 2 * rr, per
        )

    copies = exchange(n, mixed_wire, got_back, send.at[1], recv.at[1], local.at[1])
    if adjoint:
        shares = spread_parts(n, part_ref, parts, part_send, part_recv, part_local)
    for copy in copies:
        copy.wait()
    if adjoint:
        for copy in shares:
            copy.wait()
        total = parts[0]
        for d in range(1, n):
            total = total + parts[d]
        total_ref[...] = total

    pieces_of = mode_pieces(n)

    @pl.loop(0, channels // 2)
    def _(pair):
        found = [[[] for _ in range(KY)] for _ in range(2)]
        for d in range(n):
            block = got_back[d, pl.ds(pl.multiple_of(pair * 2 * rr, 16), 2 * rr), :].astype(F32)
            at = 0
            for ky, _, width in pieces_of[d]:
                for half in range(2):
                    found[half][ky].append(block[half * rr : (half + 1) * rr, at : at + width])
                at += width
        lanes = jnp.zeros((rr, LANES - KZT), F32)
        halves = [
            jnp.concatenate(
                [jnp.concatenate(found[half][ky] + [lanes], axis=1) for ky in range(KY)], axis=0
            )
            for half in range(2)
        ]
        rows_out[pair] = jnp.concatenate(halves, axis=1).astype(BF)


def mix_call(sent, weight, stream, stream_back, n, part=None):
    channels = weight.shape[1]
    rr = sent.shape[1] // channels
    per = sent.shape[2]
    adjoint = part is not None
    vmem = pl.BlockSpec(memory_space=pltpu.VMEM)
    out_shape = [
        jax.ShapeDtypeStruct((channels // 2, KY * rr, 2 * LANES), BF),
        jax.ShapeDtypeStruct((channels, 2 * KX, per), F32),
    ]
    scratch = [
        pltpu.VMEM(sent.shape, BF),
        pltpu.VMEM(weight.shape, BF),
        pltpu.VMEM(sent.shape, BF),
        pltpu.VMEM(sent.shape, BF),
        pltpu.SemaphoreType.DMA((2, n)),
        pltpu.SemaphoreType.DMA((2, n)),
        pltpu.SemaphoreType.DMA((2,)),
        pltpu.SemaphoreType.DMA(()),
    ]
    operands = [sent, weight, stream, stream_back]
    if adjoint:
        out_shape.append(jax.ShapeDtypeStruct(part.shape, F32))
        scratch += [
            pltpu.VMEM((n,) + part.shape, F32),
            pltpu.SemaphoreType.DMA((n,)),
            pltpu.SemaphoreType.DMA((n,)),
            pltpu.SemaphoreType.DMA(()),
        ]
        operands.append(part)
    return pl.pallas_call(
        partial(mix_kernel, n, rr, adjoint),
        out_shape=out_shape,
        in_specs=[vmem, pl.BlockSpec(memory_space=pl.ANY)] + [vmem] * (len(operands) - 2),
        out_specs=[vmem] * len(out_shape),
        scratch_shapes=scratch,
        compiler_params=params(40, collective_id=int(adjoint), has_side_effects=True),
        name="adjoint_mix" if adjoint else "mix",
    )(*operands)


def gelu_slope(v):
    a = jnp.abs(v)
    t = 1.0 / (1.0 + (0.3275911 * 0.7071067811865476) * a)
    e = jnp.exp(-0.5 * v * v)
    poly = 0.5 * 1.061405429
    for coefficient in (-1.453152027, 1.421413741, -0.284496736, 0.254829592):
        poly = poly * t + 0.5 * coefficient
    tail = e * (poly * t - 0.3989422804014327 * a)
    return jnp.where(v >= 0, 1.0 - tail, tail)


def planes(rows_ref, lateral, table_ref, flat, spectral, channels, cells):
    @pl.loop(0, channels // 2, unroll=5)
    def _(pair):
        both = dot(lateral, rows_ref[pair]).astype(BF)
        for half in range(2):
            at = slice(half * LANES, (half + 1) * LANES)
            plane = jnp.concatenate([both[:cells, at], both[cells:, at]], axis=1)
            flat[pl.ds(pl.multiple_of((2 * pair + half) * cells, cells), cells), :] = plane

    some = 4 * cells

    @pl.loop(0, channels // 4)
    def _(chunk):
        here = pl.ds(pl.multiple_of(chunk * some, some), some)
        out = dot(flat[here, :], table_ref[...])
        spectral[pl.ds(chunk * 4, 4)] = out.reshape((4,) + spectral.shape[1:])


def expand(channels):
    row = lax.broadcasted_iota(jnp.int32, (channels * 8, channels), 0)
    column = lax.broadcasted_iota(jnp.int32, (channels * 8, channels), 1)
    spread = ((row >= column * 8) & (row < column * 8 + 8)).astype(BF)
    wide = (channels * 8, channels * 8)
    phase = lax.broadcasted_iota(jnp.int32, wide, 0) - lax.broadcasted_iota(jnp.int32, wide, 1)
    return spread, lax.rem(phase + channels * 8, 8) == 0


def kronecker(weight, channels):
    spread, mask = expand(channels)
    wide = lax.dot_general(
        dot(spread, weight).astype(BF), spread, (((1,), (1,)), ((), ())), preferred_element_type=F32
    )
    return jnp.where(mask, wide, 0.0).astype(BF)


def middle_kernel(
    n, rr, readout_ref, bias_ref, rows_ref, field_ref, sat_ref, weight_ref, inverse_ref, back_ref,
    lat_inv_ref, lat_fwd_ref, grad_ref, wire_ref, total_ref,
    spectral, spectrum, flat, kron, readout_rows, bias_rows, corr,
):
    step = pl.program_id(0)
    channels, rows = field_ref.shape[:2]
    cells = rows * YB

    @pl.when(step == 0)
    def _():
        corr[...] = jnp.zeros_like(corr)
        spectrum[...] = jnp.zeros_like(spectrum)
        kron[...] = kronecker(weight_ref[...].astype(F32).T.astype(BF), channels)
        for o in range(channels):
            readout_rows[8 * o : 8 * o + 8, :] = jnp.full((8, LANES), readout_ref[o], F32)
            bias_rows[8 * o : 8 * o + 8, :] = jnp.full((8, LANES), bias_ref[o], F32)

    planes(rows_ref, lat_inv_ref[0], inverse_ref, flat, spectral, channels, cells)

    @pl.loop(0, rows)
    def _(x):
        lefts, rights = [], []
        for yb in range(YB // 8):
            y8 = slice(yb * 8, yb * 8 + 8)
            block = field_ref[:, x, y8, :].reshape(channels * 8, NZT)
            point = dot(kron[...], block)
            bias = jnp.concatenate([bias_rows[...]] * (NZT // LANES), axis=1)
            readout = jnp.concatenate([readout_rows[...]] * (NZT // LANES), axis=1)
            pre = point + spectral[:, x, y8, :].reshape(channels * 8, NZT) + bias
            sat = sat_ref[x, y8, :].astype(F32)
            up = readout * jnp.broadcast_to(sat[None], (channels, 8, NZT)).reshape(-1, NZT)
            grad = (up * gelu_slope(pre)).astype(BF)
            grad_ref[:, x, y8, :] = grad.reshape(channels, 8, NZT)
            lefts.append(jnp.concatenate([block, jnp.ones((16, NZT), BF)], axis=0))
            rights.append(grad)
        corr[...] += lax.dot_general(
            jnp.concatenate(lefts, axis=1),
            jnp.concatenate(rights, axis=1),
            (((1,), (1,)), ((), ())),
            preferred_element_type=F32,
        )

    some = 4 * cells

    @pl.loop(0, channels // 4)
    def _(chunk):
        grads = grad_ref[pl.ds(chunk * 4, 4)].reshape(some, NZT)
        flat[pl.ds(pl.multiple_of(chunk * some, some), some), :] = dot(grads, back_ref[...]).astype(BF)

    @pl.loop(0, channels // 2, unroll=5)
    def _(pair):
        flats = [
            flat[pl.ds(pl.multiple_of((2 * pair + half) * cells, cells), cells), :]
            for half in range(2)
        ]
        real = jnp.concatenate([f[:, :LANES] for f in flats], axis=1)
        imag = jnp.concatenate([f[:, LANES:] for f in flats], axis=1)
        spectrum[pair] += dot(lat_fwd_ref[0], jnp.concatenate([real, imag], axis=0))

    @pl.when(step == pl.num_programs(0) - 1)
    def _():
        @pl.loop(0, channels // 2)
        def _(pair):
            pack(spectrum[pair], wire_ref, pl.multiple_of(pair * 2 * rr, 16), n, rr)

        spread, mask = expand(channels)
        spread = spread.astype(F32)
        best = partial(
            lax.dot_general, preferred_element_type=F32, precision=lax.Precision.HIGHEST
        )
        sums = jnp.where(mask, corr[: channels * 8], 0.0)
        inner = best(sums, spread, (((1,), (0,)), ((), ())))
        total_ref[:channels, :] = best(spread, inner, (((0,), (0,)), ((), ())))
        total_ref[channels : channels + 4, :] = best(
            corr[channels * 8 : channels * 8 + 4], spread, (((1,), (0,)), ((), ()))
        )


def middle_call(rows_in, field, sat, readout, bias, weight, inverse, back, lat_inv, lat_fwd, n):
    channels, rows = field.shape[:2]
    rr = 2 * rows
    per = KY * KZT // n
    whole = lambda a: pl.BlockSpec(a.shape, lambda y: (0,) * a.ndim)
    scalars = pl.BlockSpec(memory_space=pltpu.SMEM)
    return pl.pallas_call(
        partial(middle_kernel, n, rr),
        grid=(NY // YB,),
        out_shape=(
            jax.ShapeDtypeStruct(field.shape, BF),
            jax.ShapeDtypeStruct((n, channels * rr, per), BF),
            jax.ShapeDtypeStruct((channels + 4, channels), F32),
        ),
        in_specs=[
            scalars, scalars,
            whole(rows_in),
            pl.BlockSpec((channels, rows, YB, NZT), lambda y: (0, 0, y, 0)),
            pl.BlockSpec((rows, YB, NZT), lambda y: (0, y, 0)),
            whole(weight), whole(inverse), whole(back),
            pl.BlockSpec((1,) + lat_inv.shape[1:], lambda y: (y, 0, 0)),
            pl.BlockSpec((1,) + lat_fwd.shape[1:], lambda y: (y, 0, 0)),
        ],
        out_specs=(
            pl.BlockSpec((channels, rows, YB, NZT), lambda y: (0, 0, y, 0)),
            pl.BlockSpec((n, channels * rr, per), lambda y: (0, 0, 0)),
            pl.BlockSpec((channels + 4, channels), lambda y: (0, 0)),
        ),
        scratch_shapes=[
            pltpu.VMEM((channels, rows, YB, NZT), F32),
            pltpu.VMEM((channels // 2, KY * rr, 2 * LANES), F32),
            pltpu.VMEM((channels * rows * YB, 2 * LANES), BF),
            pltpu.VMEM((channels * 8, channels * 8), BF),
            pltpu.VMEM((channels * 8, LANES), F32),
            pltpu.VMEM((channels * 8, LANES), F32),
            pltpu.VMEM((channels * 8 + 16, channels * 8), F32),
        ],
        compiler_params=params(58),
        name="middle",
    )(readout, bias, rows_in, field, sat, weight, inverse, back, lat_inv, lat_fwd)


def last_kernel(
    rows_ref, grad_ref, weight_ref, table_ref, lat_inv_ref, spec_ref, back_ref, total_ref,
    out_ref, outer_ref, point_ref, bias_ref, spectral, flat, kron,
):
    channels, rows = grad_ref.shape[:2]
    cells = rows * YB

    @pl.when(pl.program_id(0) == 0)
    def _():
        kron[...] = kronecker(weight_ref[...], channels)
        point_ref[...] = total_ref[:channels, :]
        bias_ref[...] = total_ref[channels : channels + 1, :]

    planes(rows_ref, lat_inv_ref[0], table_ref, flat, spectral, channels, cells)

    @pl.loop(0, rows)
    def _(x):
        for yb in range(YB // 8):
            y8 = slice(yb * 8, yb * 8 + 8)
            block = grad_ref[:, x, y8, :].reshape(channels * 8, NZT)
            total = dot(kron[...], block) + spectral[:, x, y8, :].reshape(channels * 8, NZT)
            out_ref[:, x, y8, :] = total.astype(BF).reshape(channels, 8, NZT)

    @pl.loop(0, outer_ref.shape[1])
    def _(i):
        s_real, s_imag = spec_ref[i, :KX], spec_ref[i, KX:]
        for o in range(channels):
            b_real, b_imag = back_ref[o, :KX], back_ref[o, KX:]
            outer_ref[0, i, o] = s_real * b_real + s_imag * b_imag
            outer_ref[1, i, o] = s_real * b_imag - s_imag * b_real


def last_call(rows_in, grad, weight, table, lat_inv, spec, back_spec, total):
    channels, rows = grad.shape[:2]
    per = spec.shape[2]
    steps = NY // YB
    whole = lambda a: pl.BlockSpec(a.shape, lambda y: (0,) * a.ndim)
    block = pl.BlockSpec((channels, rows, YB, NZT), lambda y: (0, 0, y, 0))
    return pl.pallas_call(
        last_kernel,
        grid=(steps,),
        out_shape=(
            jax.ShapeDtypeStruct(grad.shape, BF),
            jax.ShapeDtypeStruct((2, channels, channels, KX, per), F32),
            jax.ShapeDtypeStruct((channels, channels), F32),
            jax.ShapeDtypeStruct((1, channels), F32),
        ),
        in_specs=[
            whole(rows_in), block, whole(weight), whole(table),
            pl.BlockSpec((1,) + lat_inv.shape[1:], lambda y: (y, 0, 0)),
            pl.BlockSpec((channels // steps,) + spec.shape[1:], lambda y: (y, 0, 0)),
            whole(back_spec), whole(total),
        ],
        out_specs=(
            block,
            pl.BlockSpec((2, channels // steps, channels, KX, per), lambda y: (0, y, 0, 0, 0)),
            pl.BlockSpec((channels, channels), lambda y: (0, 0)),
            pl.BlockSpec((1, channels), lambda y: (0, 0)),
        ),
        scratch_shapes=[
            pltpu.VMEM((channels, rows, YB, NZT), F32),
            pltpu.VMEM((channels * rows * YB, 2 * LANES), BF),
            pltpu.VMEM((channels * 8, channels * 8), BF),
        ],
        compiler_params=params(58),
        name="last",
    )(rows_in, grad, weight, table, lat_inv, spec, back_spec, total)


def local(n, lifted_field, saturation_grad, readout, spectral_weight, point_weight, point_bias):
    channels, rows = lifted_field.shape[:2]
    forward_table, inverse_table = plane_tables()
    lat_fwd, lat_inv, lat_whole = lateral_tables(rows)
    stream, stream_back = stream_tables(rows * n, rows)

    sent = forward_call(lifted_field, narrow(forward_table), lat_whole, n)
    rows_in, spec = mix_call(sent, spectral_weight, stream, stream_back, n)
    grad_pre, sent_back, part = middle_call(
        rows_in, lifted_field, saturation_grad, readout, point_bias, point_weight,
        narrow(inverse_table.T), narrow(inverse_table), lat_inv, lat_fwd, n,
    )
    rows_back, back_spec, total = mix_call(sent_back, spectral_weight, stream, stream_back, n, part)
    grad_field, grad_spectral, grad_point, grad_bias = last_call(
        rows_back, grad_pre, point_weight, narrow(forward_table.T), lat_inv, spec, back_spec, total
    )
    return (grad_field, grad_spectral, grad_point, grad_bias.reshape(channels))


def solution(mesh):
    placed = (
        P(None, ("groups", "gx"), None, None),
        P(("groups", "gx"), None, None),
        P(),
        P(None, None, None, None, "gx"),
        P(),
        P(),
    )
    return jax.shard_map(
        partial(local, mesh.shape["gx"]),
        mesh=mesh,
        in_specs=placed,
        out_specs=(
            P(None, ("groups", "gx"), None, None),
            P("groups", None, None, None, "gx"),
            P("groups", None),
            P("groups"),
        ),
        check_vma=False,
    )
```

```python
from functools import partial
import math

import jax
import jax.numpy as jnp
import numpy as np
from jax import lax
from jax.experimental import pallas as pl
from jax.experimental.pallas import tpu as pltpu
from jax.sharding import PartitionSpec as P

NY = 128
NZ = 32
NT = 16
MX = 12
MY = 12
MZ = 6
MT = 4
NZT = 512
KZT = 48
KY = 2 * MY
KX = 2 * MX
LANES = 128
YB = 32
BF = jnp.bfloat16
F32 = jnp.float32
MESH = pl.DeviceIdType.MESH


def axis_tables(length, kept):
    positions = np.arange(length)
    frequency = np.concatenate([np.arange(kept), np.arange(length - kept, length)])
    angles = (frequency[:, None] * positions[None, :] % length) * (2.0 * math.pi / length)
    factor = 1.0 / math.sqrt(length)
    return np.cos(angles) * factor, np.sin(angles) * factor


def plane_tables():
    depth = np.concatenate([np.arange(MZ), np.arange(NZ - MZ, NZ)])
    phases = (
        depth[None, None, :, None] * np.arange(NZ)[:, None, None, None] * NT
        + np.arange(MT)[None, None, None, :] * np.arange(NT)[None, :, None, None] * NZ
    ) % NZT
    angles = phases * (2.0 * math.pi / NZT)
    factor = 1.0 / math.sqrt(NZT)
    cos_part = (np.cos(angles) * factor).reshape(NZT, KZT)
    sin_part = (np.sin(angles) * factor).reshape(NZT, KZT)
    weights = np.tile(np.where(np.arange(MT) == 0, 1.0, 2.0), 2 * MZ)
    forward = np.zeros((NZT, 2 * LANES))
    forward[:, :KZT], forward[:, LANES : LANES + KZT] = cos_part, -sin_part
    inverse = np.zeros((NZT, 2 * LANES))
    inverse[:, :KZT], inverse[:, LANES : LANES + KZT] = cos_part * weights, -sin_part * weights
    return forward, inverse


def narrow(table):
    return jnp.asarray(np.asarray(table, np.float32).astype(jnp.bfloat16))


def lateral_tables(rows):
    c, s = axis_tables(NY, MY)
    same = np.eye(rows)
    pairs = np.array([[c, s], [-s, c]])
    forward = np.einsum("rqky,xw->krxqwy", pairs, same)
    forward = forward.reshape(KY * 2 * rows, 2, rows, NY // YB, YB)
    forward = forward.transpose(3, 0, 1, 2, 4).reshape(NY // YB, KY * 2 * rows, 2 * rows * YB)
    inverse = np.einsum("rqky,xw->qwykrx", pairs, same)
    inverse = inverse.reshape(2, rows, NY // YB, YB, KY * 2 * rows)
    inverse = inverse.transpose(2, 0, 1, 3, 4).reshape(NY // YB, 2 * rows * YB, KY * 2 * rows)
    whole = np.einsum("rqky,xw->krxqwy", pairs, same).reshape(KY * 2 * rows, 2 * rows * NY)
    return narrow(forward), narrow(inverse), narrow(whole)


def stream_tables(cells, rows):
    c, s = axis_tables(cells, MX)
    pairs = np.array([[c, s], [-s, c]]).reshape(2, 2, KX, cells // rows, rows)
    table = np.einsum("rqkdx,ab->arkdbqx", pairs, np.eye(2))
    table = table.reshape(4 * KX, cells * 4)
    return narrow(table), narrow(table.T)


def mode_pieces(n):
    per = KY * KZT // n
    out = []
    for d in range(n):
        at, end, pieces = d * per, (d + 1) * per, []
        while at < end:
            ky, col = divmod(at, KZT)
            width = min(KZT - col, end - at)
            pieces.append((ky, col, width))
            at += width
        out.append(pieces)
    return out


def params(mib, **more):
    return pltpu.CompilerParams(vmem_limit_bytes=mib << 20, **more)


def dot(a, b):
    return jnp.dot(a, b, preferred_element_type=F32)


def pack(spectrum, out_ref, first_row, n, rr):
    for d, pieces in enumerate(mode_pieces(n)):
        halves = []
        for half in range(2):
            at = half * LANES
            parts = [
                spectrum[ky * rr : (ky + 1) * rr, at + col : at + col + width]
                for ky, col, width in pieces
            ]
            halves.append(jnp.concatenate(parts, axis=1))
        out_ref[d, pl.ds(first_row, 2 * rr), :] = jnp.concatenate(halves, axis=0).astype(BF)


def forward_kernel(n, rr, field_ref, plane_ref, lateral_ref, out_ref):
    cells = field_ref.shape[1] * NY
    flats = [
        dot(field_ref[half].reshape(cells, NZT), plane_ref[...]).astype(BF) for half in range(2)
    ]
    real = jnp.concatenate([f[:, :LANES] for f in flats], axis=1)
    imag = jnp.concatenate([f[:, LANES:] for f in flats], axis=1)
    spectrum = dot(lateral_ref[...], jnp.concatenate([real, imag], axis=0))
    pack(spectrum, out_ref, 0, n, rr)


def forward_call(field, plane_table, lateral_whole, n):
    channels, rows = field.shape[:2]
    rr = 2 * rows
    per = KY * KZT // n
    return pl.pallas_call(
        partial(forward_kernel, n, rr),
        grid=(channels // 2,),
        out_shape=jax.ShapeDtypeStruct((n, channels * rr, per), BF),
        in_specs=[
            pl.BlockSpec((2, rows, NY, NZT), lambda c: (c, 0, 0, 0)),
            pl.BlockSpec(plane_table.shape, lambda c: (0, 0)),
            pl.BlockSpec(lateral_whole.shape, lambda c: (0, 0)),
        ],
        out_specs=pl.BlockSpec((n, 2 * rr, per), lambda c: (0, c, 0)),
        compiler_params=params(60),
        name="forward",
    )(field, plane_table, lateral_whole)


def exchange(n, source, target, send, recv, local):
    me, group = lax.axis_index("gx"), lax.axis_index("groups")
    copies = []
    for k in range(1, n):
        peer = lax.rem(me + k, n)
        copy = pltpu.make_async_remote_copy(
            src_ref=source.at[peer],
            dst_ref=target.at[me],
            send_sem=send.at[k],
            recv_sem=recv.at[k],
            device_id=(group, peer),
            device_id_type=MESH,
        )
        copy.start()
        copies.append(copy)
    own = pltpu.make_async_copy(source.at[me], target.at[me], local)
    own.start()
    own.wait()
    return copies


def spread_parts(n, source, target, send, recv, local):
    me, group = lax.axis_index("gx"), lax.axis_index("groups")
    copies = []
    for k in range(1, n):
        copy = pltpu.make_async_remote_copy(
            src_ref=source,
            dst_ref=target.at[me],
            send_sem=send.at[k],
            recv_sem=recv.at[k],
            device_id=(group, lax.rem(me + k, n)),
            device_id_type=MESH,
        )
        copy.start()
        copies.append(copy)
    own = pltpu.make_async_copy(source, target.at[me], local)
    own.start()
    own.wait()
    return copies


def mix_kernel(
    n, rr, adjoint, sent, weight_hbm, field_hbm, stream_ref, back_ref, point_ref, *refs
):
    if adjoint:
        part_ref, rows_out, spec_out, mixed_hbm, total_ref, *refs = refs
        *refs, parts, part_send, part_recv, part_local = refs
    else:
        rows_out, spec_out, mixed_hbm, *refs = refs
    got, weights, mixed_wire, got_back, kron, send, recv, local, weight_sem = refs
    rows = field_hbm.shape[1]
    channels = spec_out.shape[0]
    per = spec_out.shape[2]
    me, group = lax.axis_index("gx"), lax.axis_index("groups")
    barrier = pltpu.get_barrier_semaphore()
    for k in range(1, n):
        pl.semaphore_signal(
            barrier, inc=1, device_id=(group, lax.rem(me + k, n)), device_id_type=MESH
        )
    fetch = pltpu.make_async_copy(weight_hbm, weights, weight_sem)
    fetch.start()
    pl.semaphore_wait(barrier, n - 1)
    copies = exchange(n, sent, got, send.at[0], recv.at[0], local.at[0])
    point = point_ref[...] if adjoint else point_ref[...].astype(F32).T.astype(BF)
    kron[...] = kronecker(point, channels)
    pointwise(kron, field_hbm, mixed_hbm, 0, rows // 2)
    for copy in copies:
        copy.wait()

    @pl.loop(0, channels // 2)
    def _(pair):
        block = got[:, pl.ds(pl.multiple_of(pair * 2 * rr, 16), 2 * rr), :]
        both = dot(stream_ref[...], block.reshape(n * 2 * rr, per))
        spec_out[2 * pair] = both[: 2 * KX]
        spec_out[2 * pair + 1] = both[2 * KX :]

    fetch.wait()

    @pl.loop(0, channels // 2)
    def _(pair):
        results = []
        for half in range(2):
            o = 2 * pair + half
            real = jnp.zeros((KX, per), F32)
            imag = jnp.zeros((KX, per), F32)
            for i in range(channels):
                at = (o, i) if adjoint else (i, o)
                w_real = weights[0, at[0], at[1]].astype(F32)
                w_imag = weights[1, at[0], at[1]].astype(F32)
                s_real = spec_out[i, :KX]
                s_imag = spec_out[i, KX:]
                if adjoint:
                    real += w_real * s_real + w_imag * s_imag
                    imag += w_real * s_imag - w_imag * s_real
                else:
                    real += w_real * s_real - w_imag * s_imag
                    imag += w_real * s_imag + w_imag * s_real
            results += [real, imag]
        both = dot(back_ref[...], jnp.concatenate(results, axis=0).astype(BF)).astype(BF)
        mixed_wire[:, pl.ds(pl.multiple_of(pair * 2 * rr, 16), 2 * rr), :] = both.reshape(
            n, 2 * rr, per
        )

    copies = exchange(n, mixed_wire, got_back, send.at[1], recv.at[1], local.at[1])
    if adjoint:
        shares = spread_parts(n, part_ref, parts, part_send, part_recv, part_local)
    pointwise(kron, field_hbm, mixed_hbm, rows // 2, rows - rows // 2)
    for copy in copies:
        copy.wait()
    if adjoint:
        for copy in shares:
            copy.wait()
        total = parts[0]
        for d in range(1, n):
            total = total + parts[d]
        total_ref[...] = total

    pieces_of = mode_pieces(n)

    @pl.loop(0, channels // 2)
    def _(pair):
        found = [[[] for _ in range(KY)] for _ in range(2)]
        for d in range(n):
            block = got_back[d, pl.ds(pl.multiple_of(pair * 2 * rr, 16), 2 * rr), :].astype(F32)
            at = 0
            for ky, _, width in pieces_of[d]:
                for half in range(2):
                    found[half][ky].append(block[half * rr : (half + 1) * rr, at : at + width])
                at += width
        lanes = jnp.zeros((rr, LANES - KZT), F32)
        halves = [
            jnp.concatenate(
                [jnp.concatenate(found[half][ky] + [lanes], axis=1) for ky in range(KY)], axis=0
            )
            for half in range(2)
        ]
        rows_out[pair] = jnp.concatenate(halves, axis=1).astype(BF)


def mix_call(sent, weight, field, stream, stream_back, point, n, part=None):
    channels = weight.shape[1]
    rr = sent.shape[1] // channels
    per = sent.shape[2]
    adjoint = part is not None
    vmem = pl.BlockSpec(memory_space=pltpu.VMEM)
    out_shape = [
        jax.ShapeDtypeStruct((channels // 2, KY * rr, 2 * LANES), BF),
        jax.ShapeDtypeStruct((channels, 2 * KX, per), F32),
        jax.ShapeDtypeStruct(field.shape, BF),
    ]
    hbm = pl.BlockSpec(memory_space=pl.ANY)
    scratch = [
        pltpu.VMEM(sent.shape, BF),
        pltpu.VMEM(weight.shape, BF),
        pltpu.VMEM(sent.shape, BF),
        pltpu.VMEM(sent.shape, BF),
        pltpu.VMEM((channels * 8, channels * 8), BF),
        pltpu.SemaphoreType.DMA((2, n)),
        pltpu.SemaphoreType.DMA((2, n)),
        pltpu.SemaphoreType.DMA((2,)),
        pltpu.SemaphoreType.DMA(()),
    ]
    operands = [sent, weight, field, stream, stream_back, point]
    if adjoint:
        out_shape.append(jax.ShapeDtypeStruct(part.shape, F32))
        scratch += [
            pltpu.VMEM((n,) + part.shape, F32),
            pltpu.SemaphoreType.DMA((n,)),
            pltpu.SemaphoreType.DMA((n,)),
            pltpu.SemaphoreType.DMA(()),
        ]
        operands.append(part)
    return pl.pallas_call(
        partial(mix_kernel, n, rr, adjoint),
        out_shape=out_shape,
        in_specs=[vmem, hbm, hbm] + [vmem] * (len(operands) - 3),
        out_specs=[vmem, vmem, hbm] + [vmem] * (len(out_shape) - 3),
        scratch_shapes=scratch,
        compiler_params=params(58, collective_id=int(adjoint), has_side_effects=True),
        name="adjoint_mix" if adjoint else "mix",
    )(*operands)


def gelu_slope(v):
    cumulative = 0.5 + 0.5 * lax.erf(v * 0.7071067811865476)
    return cumulative + v * (jnp.exp(-0.5 * v * v) * 0.3989422804014327)


def planes(rows_ref, lateral, flat, channels, cells):
    @pl.loop(0, channels // 2, unroll=5)
    def _(pair):
        both = dot(lateral, rows_ref[pair]).astype(BF)
        for half in range(2):
            at = slice(half * LANES, (half + 1) * LANES)
            plane = jnp.concatenate([both[:cells, at], both[cells:, at]], axis=1)
            flat[pl.ds(pl.multiple_of((2 * pair + half) * cells, cells), cells), :] = plane


def pointwise(kron, source, target, first, count):
    channels = source.shape[0]

    def body(block_ref, out_ref):
        for yb in range(YB // 8):
            y8 = slice(yb * 8, yb * 8 + 8)
            block = block_ref[:, 0, y8, :].reshape(channels * 8, NZT)
            out_ref[:, 0, y8, :] = dot(kron[...], block).astype(BF).reshape(channels, 8, NZT)

    spec = pl.BlockSpec((channels, 1, YB, NZT), lambda x, y: (0, first + x, y, 0))
    pltpu.emit_pipeline(body, grid=(count, NY // YB), in_specs=[spec], out_specs=[spec])(
        source, target
    )


def expand(channels):
    row = lax.broadcasted_iota(jnp.int32, (channels * 8, channels), 0)
    column = lax.broadcasted_iota(jnp.int32, (channels * 8, channels), 1)
    spread = ((row >= column * 8) & (row < column * 8 + 8)).astype(BF)
    wide = (channels * 8, channels * 8)
    phase = lax.broadcasted_iota(jnp.int32, wide, 0) - lax.broadcasted_iota(jnp.int32, wide, 1)
    return spread, lax.rem(phase + channels * 8, 8) == 0


def kronecker(weight, channels):
    spread, mask = expand(channels)
    wide = lax.dot_general(
        dot(spread, weight).astype(BF), spread, (((1,), (1,)), ((), ())), preferred_element_type=F32
    )
    return jnp.where(mask, wide, 0.0).astype(BF)


def middle_kernel(
    n, rr, readout_ref, bias_ref, rows_ref, field_ref, point_ref, sat_ref, inverse_ref, back_ref,
    lat_inv_ref, lat_fwd_ref, grad_ref, wire_ref, total_ref, spectrum, flat, corr,
):
    step = pl.program_id(0)
    channels, rows = field_ref.shape[:2]
    cells = rows * YB

    @pl.when(step == 0)
    def _():
        corr[...] = jnp.zeros_like(corr)
        spectrum[...] = jnp.zeros_like(spectrum)

    planes(rows_ref, lat_inv_ref[0], flat, channels, cells)

    @pl.loop(0, channels // 2)
    def _(pair):
        here = pl.ds(pl.multiple_of(pair * 2 * cells, 2 * cells), 2 * cells)
        both = dot(flat[here, :], inverse_ref[...])
        sat = sat_ref[...].reshape(cells, NZT).astype(F32)
        for half in range(2):
            o = 2 * pair + half
            pre = both[half * cells : (half + 1) * cells]
            pre = pre + point_ref[o].reshape(cells, NZT).astype(F32) + bias_ref[o]
            grad = (readout_ref[o] * sat * gelu_slope(pre)).astype(BF)
            grad_ref[o] = grad.reshape(rows, YB, NZT)

    @pl.loop(0, rows)
    def _(x):
        lefts, rights = [], []
        for yb in range(YB // 8):
            y8 = slice(yb * 8, yb * 8 + 8)
            block = field_ref[:, x, y8, :].reshape(channels * 8, NZT)
            lefts.append(jnp.concatenate([block, jnp.ones((16, NZT), BF)], axis=0))
            rights.append(grad_ref[:, x, y8, :].reshape(channels * 8, NZT))
        corr[...] += lax.dot_general(
            jnp.concatenate(lefts, axis=1),
            jnp.concatenate(rights, axis=1),
            (((1,), (1,)), ((), ())),
            preferred_element_type=F32,
        )

    some = 4 * cells

    @pl.loop(0, channels // 4)
    def _(chunk):
        grads = grad_ref[pl.ds(chunk * 4, 4)].reshape(some, NZT)
        flat[pl.ds(pl.multiple_of(chunk * some, some), some), :] = dot(grads, back_ref[...]).astype(BF)

    @pl.loop(0, channels // 2, unroll=5)
    def _(pair):
        flats = [
            flat[pl.ds(pl.multiple_of((2 * pair + half) * cells, cells), cells), :]
            for half in range(2)
        ]
        real = jnp.concatenate([f[:, :LANES] for f in flats], axis=1)
        imag = jnp.concatenate([f[:, LANES:] for f in flats], axis=1)
        spectrum[pair] += dot(lat_fwd_ref[0], jnp.concatenate([real, imag], axis=0))

    @pl.when(step == pl.num_programs(0) - 1)
    def _():
        @pl.loop(0, channels // 2)
        def _(pair):
            pack(spectrum[pair], wire_ref, pl.multiple_of(pair * 2 * rr, 16), n, rr)

        spread, mask = expand(channels)
        spread = spread.astype(F32)
        best = partial(
            lax.dot_general, preferred_element_type=F32, precision=lax.Precision.HIGHEST
        )
        sums = jnp.where(mask, corr[: channels * 8], 0.0)
        inner = best(sums, spread, (((1,), (0,)), ((), ())))
        total_ref[...] = jnp.zeros_like(total_ref)
        total_ref[:channels, :channels] = best(spread, inner, (((0,), (0,)), ((), ())))
        total_ref[channels : channels + 4, :channels] = best(
            corr[channels * 8 : channels * 8 + 4], spread, (((1,), (0,)), ((), ()))
        )


def middle_call(rows_in, field, point, sat, readout, bias, inverse, back, lat_inv, lat_fwd, n):
    channels, rows = field.shape[:2]
    rr = 2 * rows
    per = KY * KZT // n
    whole = lambda a: pl.BlockSpec(a.shape, lambda y: (0,) * a.ndim)
    scalars = pl.BlockSpec(memory_space=pltpu.SMEM)
    return pl.pallas_call(
        partial(middle_kernel, n, rr),
        grid=(NY // YB,),
        out_shape=(
            jax.ShapeDtypeStruct(field.shape, BF),
            jax.ShapeDtypeStruct((n, channels * rr, per), BF),
            jax.ShapeDtypeStruct((channels + 4, LANES), F32),
        ),
        in_specs=[
            scalars, scalars,
            whole(rows_in),
            pl.BlockSpec((channels, rows, YB, NZT), lambda y: (0, 0, y, 0)),
            pl.BlockSpec((channels, rows, YB, NZT), lambda y: (0, 0, y, 0)),
            pl.BlockSpec((rows, YB, NZT), lambda y: (0, y, 0)),
            whole(inverse), whole(back),
            pl.BlockSpec((1,) + lat_inv.shape[1:], lambda y: (y, 0, 0)),
            pl.BlockSpec((1,) + lat_fwd.shape[1:], lambda y: (y, 0, 0)),
        ],
        out_specs=(
            pl.BlockSpec((channels, rows, YB, NZT), lambda y: (0, 0, y, 0)),
            pl.BlockSpec((n, channels * rr, per), lambda y: (0, 0, 0)),
            pl.BlockSpec((channels + 4, LANES), lambda y: (0, 0)),
        ),
        scratch_shapes=[
            pltpu.VMEM((channels // 2, KY * rr, 2 * LANES), F32),
            pltpu.VMEM((channels * rows * YB, 2 * LANES), BF),
            pltpu.VMEM((channels * 8 + 16, channels * 8), F32),
        ],
        compiler_params=params(58),
        name="middle",
    )(readout, bias, rows_in, field, point, sat, inverse, back, lat_inv, lat_fwd)


def last_kernel(
    rows_ref, grad_ref, table_ref, lat_inv_ref, spec_ref, back_ref, total_ref,
    out_ref, outer_ref, point_ref, bias_ref, flat,
):
    channels, rows = grad_ref.shape[:2]
    cells = rows * YB

    @pl.when(pl.program_id(0) == 0)
    def _():
        point_ref[...] = total_ref[:channels, :channels]
        bias_ref[...] = total_ref[channels : channels + 1, :channels]

    planes(rows_ref, lat_inv_ref[0], flat, channels, cells)

    @pl.loop(0, channels // 4)
    def _(chunk):
        here = pl.ds(pl.multiple_of(chunk * 4 * cells, 4 * cells), 4 * cells)
        spectral = dot(flat[here, :], table_ref[...]).reshape(4, rows, YB, NZT)
        some = pl.ds(chunk * 4, 4)
        out_ref[some] = (spectral + grad_ref[some].astype(F32)).astype(BF)

    @pl.loop(0, outer_ref.shape[1])
    def _(i):
        s_real, s_imag = spec_ref[i, :KX], spec_ref[i, KX:]
        for o in range(channels):
            b_real, b_imag = back_ref[o, :KX], back_ref[o, KX:]
            outer_ref[0, i, o] = s_real * b_real + s_imag * b_imag
            outer_ref[1, i, o] = s_real * b_imag - s_imag * b_real


def last_call(rows_in, grad, table, lat_inv, spec, back_spec, total):
    channels, rows = grad.shape[:2]
    per = spec.shape[2]
    steps = NY // YB
    whole = lambda a: pl.BlockSpec(a.shape, lambda y: (0,) * a.ndim)
    block = pl.BlockSpec((channels, rows, YB, NZT), lambda y: (0, 0, y, 0))
    return pl.pallas_call(
        last_kernel,
        grid=(steps,),
        out_shape=(
            jax.ShapeDtypeStruct(grad.shape, BF),
            jax.ShapeDtypeStruct((2, channels, channels, KX, per), F32),
            jax.ShapeDtypeStruct((channels, channels), F32),
            jax.ShapeDtypeStruct((1, channels), F32),
        ),
        in_specs=[
            whole(rows_in), block, whole(table),
            pl.BlockSpec((1,) + lat_inv.shape[1:], lambda y: (y, 0, 0)),
            pl.BlockSpec((channels // steps,) + spec.shape[1:], lambda y: (y, 0, 0)),
            whole(back_spec), whole(total),
        ],
        out_specs=(
            block,
            pl.BlockSpec((2, channels // steps, channels, KX, per), lambda y: (0, y, 0, 0, 0)),
            pl.BlockSpec((channels, channels), lambda y: (0, 0)),
            pl.BlockSpec((1, channels), lambda y: (0, 0)),
        ),
        scratch_shapes=[
            pltpu.VMEM((channels * rows * YB, 2 * LANES), BF),
        ],
        compiler_params=params(58),
        name="last",
    )(rows_in, grad, table, lat_inv, spec, back_spec, total)


def local(n, lifted_field, saturation_grad, readout, spectral_weight, point_weight, point_bias):
    channels, rows = lifted_field.shape[:2]
    forward_table, inverse_table = plane_tables()
    lat_fwd, lat_inv, lat_whole = lateral_tables(rows)
    stream, stream_back = stream_tables(rows * n, rows)

    sent = forward_call(lifted_field, narrow(forward_table), lat_whole, n)
    rows_in, spec, point_term = mix_call(
        sent, spectral_weight, lifted_field, stream, stream_back, point_weight, n
    )
    grad_pre, sent_back, part = middle_call(
        rows_in, lifted_field, point_term, saturation_grad, readout, point_bias,
        narrow(inverse_table.T), narrow(inverse_table), lat_inv, lat_fwd, n,
    )
    rows_back, back_spec, point_in, total = mix_call(
        sent_back, spectral_weight, grad_pre, stream, stream_back, point_weight, n, part
    )
    grad_field, grad_spectral, grad_point, grad_bias = last_call(
        rows_back, point_in, narrow(forward_table.T), lat_inv, spec, back_spec, total
    )
    return (grad_field, grad_spectral, grad_point, grad_bias.reshape(channels))


def solution(mesh):
    placed = (
        P(None, ("groups", "gx"), None, None),
        P(("groups", "gx"), None, None),
        P(),
        P(None, None, None, None, "gx"),
        P(),
        P(),
    )
    return jax.shard_map(
        partial(local, mesh.shape["gx"]),
        mesh=mesh,
        in_specs=placed,
        out_specs=(
            P(None, ("groups", "gx"), None, None),
            P("groups", None, None, None, "gx"),
            P("groups", None),
            P("groups"),
        ),
        check_vma=False,
    )
```

```python
from functools import partial
import math

import jax
import jax.numpy as jnp
import numpy as np
from jax import lax
from jax.experimental import pallas as pl
from jax.experimental.pallas import tpu as pltpu
from jax.sharding import PartitionSpec as P

NY = 128
NZ = 32
NT = 16
MX = 12
MY = 12
MZ = 6
MT = 4
NZT = 512
KZT = 48
KY = 2 * MY
KX = 2 * MX
LANES = 128
YB = 32
BF = jnp.bfloat16
F32 = jnp.float32
MESH = pl.DeviceIdType.MESH


def axis_tables(length, kept):
    positions = np.arange(length)
    frequency = np.concatenate([np.arange(kept), np.arange(length - kept, length)])
    angles = (frequency[:, None] * positions[None, :] % length) * (2.0 * math.pi / length)
    factor = 1.0 / math.sqrt(length)
    return np.cos(angles) * factor, np.sin(angles) * factor


def plane_tables():
    depth = np.concatenate([np.arange(MZ), np.arange(NZ - MZ, NZ)])
    phases = (
        depth[None, None, :, None] * np.arange(NZ)[:, None, None, None] * NT
        + np.arange(MT)[None, None, None, :] * np.arange(NT)[None, :, None, None] * NZ
    ) % NZT
    angles = phases * (2.0 * math.pi / NZT)
    factor = 1.0 / math.sqrt(NZT)
    cos_part = (np.cos(angles) * factor).reshape(NZT, KZT)
    sin_part = (np.sin(angles) * factor).reshape(NZT, KZT)
    weights = np.tile(np.where(np.arange(MT) == 0, 1.0, 2.0), 2 * MZ)
    forward = np.zeros((NZT, 2 * LANES))
    forward[:, :KZT], forward[:, LANES : LANES + KZT] = cos_part, -sin_part
    inverse = np.zeros((NZT, 2 * LANES))
    inverse[:, :KZT], inverse[:, LANES : LANES + KZT] = cos_part * weights, -sin_part * weights
    return forward, inverse


def narrow(table):
    return jnp.asarray(np.asarray(table, np.float32).astype(jnp.bfloat16))


def lateral_tables(rows):
    c, s = axis_tables(NY, MY)
    same = np.eye(rows)
    pairs = np.array([[c, s], [-s, c]])
    forward = np.einsum("rqky,xw->krxqwy", pairs, same)
    forward = forward.reshape(KY * 2 * rows, 2, rows, NY // YB, YB)
    forward = forward.transpose(3, 0, 1, 2, 4).reshape(NY // YB, KY * 2 * rows, 2 * rows * YB)
    inverse = np.einsum("rqky,xw->qwykrx", pairs, same)
    inverse = inverse.reshape(2, rows, NY // YB, YB, KY * 2 * rows)
    inverse = inverse.transpose(2, 0, 1, 3, 4).reshape(NY // YB, 2 * rows * YB, KY * 2 * rows)
    whole = np.einsum("rqky,xw->krxqwy", pairs, same).reshape(KY * 2 * rows, 2 * rows * NY)
    return narrow(forward), narrow(inverse), narrow(whole)


def stream_tables(cells, rows):
    c, s = axis_tables(cells, MX)
    pairs = np.array([[c, s], [-s, c]]).reshape(2, 2, KX, cells // rows, rows)
    table = np.einsum("rqkdx,ab->arkdbqx", pairs, np.eye(2))
    table = table.reshape(4 * KX, cells * 4)
    return narrow(table), narrow(table.T)


def mode_pieces(n):
    per = KY * KZT // n
    out = []
    for d in range(n):
        at, end, pieces = d * per, (d + 1) * per, []
        while at < end:
            ky, col = divmod(at, KZT)
            width = min(KZT - col, end - at)
            pieces.append((ky, col, width))
            at += width
        out.append(pieces)
    return out


def params(mib, **more):
    return pltpu.CompilerParams(vmem_limit_bytes=mib << 20, **more)


def dot(a, b):
    return jnp.dot(a, b, preferred_element_type=F32)


def pack(spectrum, out_ref, first_row, n, rr):
    for d, pieces in enumerate(mode_pieces(n)):
        halves = []
        for half in range(2):
            at = half * LANES
            parts = [
                spectrum[ky * rr : (ky + 1) * rr, at + col : at + col + width]
                for ky, col, width in pieces
            ]
            halves.append(jnp.concatenate(parts, axis=1))
        out_ref[d, pl.ds(first_row, 2 * rr), :] = jnp.concatenate(halves, axis=0).astype(BF)


def forward_kernel(n, rr, field_ref, plane_ref, lateral_ref, out_ref):
    cells = field_ref.shape[1] * NY
    flats = [
        dot(field_ref[half].reshape(cells, NZT), plane_ref[...]).astype(BF) for half in range(2)
    ]
    real = jnp.concatenate([f[:, :LANES] for f in flats], axis=1)
    imag = jnp.concatenate([f[:, LANES:] for f in flats], axis=1)
    spectrum = dot(lateral_ref[...], jnp.concatenate([real, imag], axis=0))
    pack(spectrum, out_ref, 0, n, rr)


def forward_part(n, rr, field_hbm, plane_ref, lateral_ref, sent, first, count):
    rows = field_hbm.shape[1]
    per = sent.shape[2]
    pltpu.emit_pipeline(
        lambda field_ref, out_ref: forward_kernel(
            n, rr, field_ref, plane_ref, lateral_ref, out_ref
        ),
        grid=(count,),
        in_specs=[pl.BlockSpec((2, rows, NY, NZT), lambda c: (c + first, 0, 0, 0))],
        out_specs=[pl.BlockSpec((n, 2 * rr, per), lambda c: (0, c + first, 0))],
    )(field_hbm, sent)


def exchange(n, source, target, send, recv, local, first, count):
    me, group = lax.axis_index("gx"), lax.axis_index("groups")
    rows = pl.ds(first, count)
    copies = []
    for k in range(1, n):
        peer = lax.rem(me + k, n)
        copy = pltpu.make_async_remote_copy(
            src_ref=source.at[peer, rows],
            dst_ref=target.at[me, rows],
            send_sem=send.at[k],
            recv_sem=recv.at[k],
            device_id=(group, peer),
            device_id_type=MESH,
        )
        copy.start()
        copies.append(copy)
    own = pltpu.make_async_copy(source.at[me, rows], target.at[me, rows], local)
    own.start()
    return copies + [own]


def spread_parts(n, source, target, send, recv, local):
    me, group = lax.axis_index("gx"), lax.axis_index("groups")
    copies = []
    for k in range(1, n):
        copy = pltpu.make_async_remote_copy(
            src_ref=source,
            dst_ref=target.at[me],
            send_sem=send.at[k],
            recv_sem=recv.at[k],
            device_id=(group, lax.rem(me + k, n)),
            device_id_type=MESH,
        )
        copy.start()
        copies.append(copy)
    own = pltpu.make_async_copy(source, target.at[me], local)
    own.start()
    return copies + [own]


def mix_kernel(n, rr, adjoint, weight_hbm, field_hbm, stream_ref, back_ref, point_ref, *refs):
    if adjoint:
        sent, part_ref, rows_out, spec_out, mixed_hbm, total_ref, *refs = refs
        *refs, parts, part_send, part_recv, part_local = refs
    else:
        plane_ref, lateral_ref, rows_out, spec_out, mixed_hbm, *refs = refs
        *refs, sent = refs
    got, weights, mixed_wire, got_back, kron, send, recv, local, weight_sem = refs
    rows = field_hbm.shape[1]
    channels = spec_out.shape[0]
    per = spec_out.shape[2]
    pairs = channels // 2
    early = pairs // 2
    me, group = lax.axis_index("gx"), lax.axis_index("groups")
    barrier = pltpu.get_barrier_semaphore()
    for k in range(1, n):
        pl.semaphore_signal(
            barrier, inc=1, device_id=(group, lax.rem(me + k, n)), device_id_type=MESH
        )
    fetch = pltpu.make_async_copy(weight_hbm, weights, weight_sem)
    fetch.start()

    def out(source, target, slot, first, count):
        return exchange(
            n, source, target, send.at[slot], recv.at[slot], local.at[slot],
            first * 2 * rr, count * 2 * rr,
        )

    if adjoint:
        pl.semaphore_wait(barrier, n - 1)
        copies = out(sent, got, 0, 0, pairs)
        shares = spread_parts(n, part_ref, parts, part_send, part_recv, part_local)
    else:
        forward_part(n, rr, field_hbm, plane_ref, lateral_ref, sent, 0, early)
        pl.semaphore_wait(barrier, n - 1)
        copies = out(sent, got, 0, 0, early)
        forward_part(n, rr, field_hbm, plane_ref, lateral_ref, sent, early, pairs - early)
        copies += out(sent, got, 1, early, pairs - early)
        shares = []
    point = point_ref[...] if adjoint else point_ref[...].astype(F32).T.astype(BF)
    kron[...] = kronecker(point, channels)
    pointwise(kron, field_hbm, mixed_hbm, 0, rows // 2)
    for copy in copies:
        copy.wait()

    @pl.loop(0, pairs)
    def _(pair):
        block = got[:, pl.ds(pl.multiple_of(pair * 2 * rr, 16), 2 * rr), :]
        both = dot(stream_ref[...], block.reshape(n * 2 * rr, per))
        spec_out[2 * pair] = both[: 2 * KX]
        spec_out[2 * pair + 1] = both[2 * KX :]

    fetch.wait()

    def mix(pair):
        results = []
        for half in range(2):
            o = 2 * pair + half
            real = jnp.zeros((KX, per), F32)
            imag = jnp.zeros((KX, per), F32)
            for i in range(channels):
                at = (o, i) if adjoint else (i, o)
                w_real = weights[0, at[0], at[1]].astype(F32)
                w_imag = weights[1, at[0], at[1]].astype(F32)
                s_real = spec_out[i, :KX]
                s_imag = spec_out[i, KX:]
                if adjoint:
                    real += w_real * s_real + w_imag * s_imag
                    imag += w_real * s_imag - w_imag * s_real
                else:
                    real += w_real * s_real - w_imag * s_imag
                    imag += w_real * s_imag + w_imag * s_real
            results += [real, imag]
        both = dot(back_ref[...], jnp.concatenate(results, axis=0).astype(BF)).astype(BF)
        mixed_wire[:, pl.ds(pl.multiple_of(pair * 2 * rr, 16), 2 * rr), :] = both.reshape(
            n, 2 * rr, per
        )

    pl.loop(0, early)(mix)
    copies = out(mixed_wire, got_back, 2, 0, early)
    pl.loop(early, pairs)(mix)
    copies += out(mixed_wire, got_back, 3, early, pairs - early)
    pointwise(kron, field_hbm, mixed_hbm, rows // 2, rows - rows // 2)
    for copy in copies + shares:
        copy.wait()
    if adjoint:
        total = parts[0]
        for d in range(1, n):
            total = total + parts[d]
        total_ref[...] = total

    pieces_of = mode_pieces(n)

    @pl.loop(0, channels // 2)
    def _(pair):
        found = [[[] for _ in range(KY)] for _ in range(2)]
        for d in range(n):
            block = got_back[d, pl.ds(pl.multiple_of(pair * 2 * rr, 16), 2 * rr), :].astype(F32)
            at = 0
            for ky, _, width in pieces_of[d]:
                for half in range(2):
                    found[half][ky].append(block[half * rr : (half + 1) * rr, at : at + width])
                at += width
        lanes = jnp.zeros((rr, LANES - KZT), F32)
        halves = [
            jnp.concatenate(
                [jnp.concatenate(found[half][ky] + [lanes], axis=1) for ky in range(KY)], axis=0
            )
            for half in range(2)
        ]
        rows_out[pair] = jnp.concatenate(halves, axis=1).astype(BF)


def mix_call(weight, field, stream, stream_back, point, n, sent=None, part=None, tables=None):
    channels, rows = field.shape[:2]
    rr = 2 * rows
    per = weight.shape[4]
    adjoint = sent is not None
    wire = (n, channels * rr, per)
    vmem = pl.BlockSpec(memory_space=pltpu.VMEM)
    hbm = pl.BlockSpec(memory_space=pl.ANY)
    out_shape = [
        jax.ShapeDtypeStruct((channels // 2, KY * rr, 2 * LANES), BF),
        jax.ShapeDtypeStruct((channels, 2 * KX, per), F32),
        jax.ShapeDtypeStruct(field.shape, BF),
    ]
    scratch = [
        pltpu.VMEM(wire, BF),
        pltpu.VMEM(weight.shape, BF),
        pltpu.VMEM(wire, BF),
        pltpu.VMEM(wire, BF),
        pltpu.VMEM((channels * 8, channels * 8), BF),
        pltpu.SemaphoreType.DMA((4, n)),
        pltpu.SemaphoreType.DMA((4, n)),
        pltpu.SemaphoreType.DMA((4,)),
        pltpu.SemaphoreType.DMA(()),
    ]
    operands = [weight, field, stream, stream_back, point]
    if adjoint:
        out_shape.append(jax.ShapeDtypeStruct(part.shape, F32))
        scratch += [
            pltpu.VMEM((n,) + part.shape, F32),
            pltpu.SemaphoreType.DMA((n,)),
            pltpu.SemaphoreType.DMA((n,)),
            pltpu.SemaphoreType.DMA(()),
        ]
        operands += [sent, part]
    else:
        scratch.append(pltpu.VMEM(wire, BF))
        operands += list(tables)
    return pl.pallas_call(
        partial(mix_kernel, n, rr, adjoint),
        out_shape=out_shape,
        in_specs=[hbm, hbm] + [vmem] * (len(operands) - 2),
        out_specs=[vmem, vmem, hbm] + [vmem] * (len(out_shape) - 3),
        scratch_shapes=scratch,
        compiler_params=params(58, collective_id=int(adjoint), has_side_effects=True),
        name="adjoint_mix" if adjoint else "forward_mix",
    )(*operands)


def gelu_slope(v):
    cumulative = 0.5 + 0.5 * lax.erf(v * 0.7071067811865476)
    return cumulative + v * (jnp.exp(-0.5 * v * v) * 0.3989422804014327)


def planes(rows_ref, lateral, flat, channels, cells):
    @pl.loop(0, channels // 2, unroll=5)
    def _(pair):
        both = dot(lateral, rows_ref[pair]).astype(BF)
        for half in range(2):
            at = slice(half * LANES, (half + 1) * LANES)
            plane = jnp.concatenate([both[:cells, at], both[cells:, at]], axis=1)
            flat[pl.ds(pl.multiple_of((2 * pair + half) * cells, cells), cells), :] = plane


def pointwise(kron, source, target, first, count):
    channels = source.shape[0]

    def body(block_ref, out_ref):
        for yb in range(YB // 8):
            y8 = slice(yb * 8, yb * 8 + 8)
            block = block_ref[:, 0, y8, :].reshape(channels * 8, NZT)
            out_ref[:, 0, y8, :] = dot(kron[...], block).astype(BF).reshape(channels, 8, NZT)

    spec = pl.BlockSpec((channels, 1, YB, NZT), lambda x, y: (0, first + x, y, 0))
    pltpu.emit_pipeline(body, grid=(count, NY // YB), in_specs=[spec], out_specs=[spec])(
        source, target
    )


def expand(channels):
    row = lax.broadcasted_iota(jnp.int32, (channels * 8, channels), 0)
    column = lax.broadcasted_iota(jnp.int32, (channels * 8, channels), 1)
    spread = ((row >= column * 8) & (row < column * 8 + 8)).astype(BF)
    wide = (channels * 8, channels * 8)
    phase = lax.broadcasted_iota(jnp.int32, wide, 0) - lax.broadcasted_iota(jnp.int32, wide, 1)
    return spread, lax.rem(phase + channels * 8, 8) == 0


def kronecker(weight, channels):
    spread, mask = expand(channels)
    wide = lax.dot_general(
        dot(spread, weight).astype(BF), spread, (((1,), (1,)), ((), ())), preferred_element_type=F32
    )
    return jnp.where(mask, wide, 0.0).astype(BF)


def middle_kernel(
    n, rr, readout_ref, bias_ref, rows_ref, field_ref, point_ref, sat_ref, inverse_ref, back_ref,
    lat_inv_ref, lat_fwd_ref, grad_ref, wire_ref, total_ref, spectrum, flat, corr,
):
    step = pl.program_id(0)
    channels, rows = field_ref.shape[:2]
    cells = rows * YB

    @pl.when(step == 0)
    def _():
        corr[...] = jnp.zeros_like(corr)
        spectrum[...] = jnp.zeros_like(spectrum)

    planes(rows_ref, lat_inv_ref[0], flat, channels, cells)

    @pl.loop(0, channels // 2)
    def _(pair):
        here = pl.ds(pl.multiple_of(pair * 2 * cells, 2 * cells), 2 * cells)
        both = dot(flat[here, :], inverse_ref[...])
        sat = sat_ref[...].reshape(cells, NZT).astype(F32)
        for half in range(2):
            o = 2 * pair + half
            pre = both[half * cells : (half + 1) * cells]
            pre = pre + point_ref[o].reshape(cells, NZT).astype(F32) + bias_ref[o]
            grad = (readout_ref[o] * sat * gelu_slope(pre)).astype(BF)
            grad_ref[o] = grad.reshape(rows, YB, NZT)

    @pl.loop(0, rows)
    def _(x):
        lefts, rights = [], []
        for yb in range(YB // 8):
            y8 = slice(yb * 8, yb * 8 + 8)
            block = field_ref[:, x, y8, :].reshape(channels * 8, NZT)
            lefts.append(jnp.concatenate([block, jnp.ones((16, NZT), BF)], axis=0))
            rights.append(grad_ref[:, x, y8, :].reshape(channels * 8, NZT))
        corr[...] += lax.dot_general(
            jnp.concatenate(lefts, axis=1),
            jnp.concatenate(rights, axis=1),
            (((1,), (1,)), ((), ())),
            preferred_element_type=F32,
        )

    some = 4 * cells

    @pl.loop(0, channels // 4)
    def _(chunk):
        grads = grad_ref[pl.ds(chunk * 4, 4)].reshape(some, NZT)
        flat[pl.ds(pl.multiple_of(chunk * some, some), some), :] = dot(grads, back_ref[...]).astype(BF)

    @pl.loop(0, channels // 2, unroll=5)
    def _(pair):
        flats = [
            flat[pl.ds(pl.multiple_of((2 * pair + half) * cells, cells), cells), :]
            for half in range(2)
        ]
        real = jnp.concatenate([f[:, :LANES] for f in flats], axis=1)
        imag = jnp.concatenate([f[:, LANES:] for f in flats], axis=1)
        spectrum[pair] += dot(lat_fwd_ref[0], jnp.concatenate([real, imag], axis=0))

    @pl.when(step == pl.num_programs(0) - 1)
    def _():
        @pl.loop(0, channels // 2)
        def _(pair):
            pack(spectrum[pair], wire_ref, pl.multiple_of(pair * 2 * rr, 16), n, rr)

        spread, mask = expand(channels)
        spread = spread.astype(F32)
        best = partial(
            lax.dot_general, preferred_element_type=F32, precision=lax.Precision.HIGHEST
        )
        sums = jnp.where(mask, corr[: channels * 8], 0.0)
        inner = best(sums, spread, (((1,), (0,)), ((), ())))
        point = best(spread, inner, (((0,), (0,)), ((), ())))
        bias = best(corr[channels * 8 : channels * 8 + 8], spread, (((1,), (0,)), ((), ())))
        total_ref[...] = jnp.zeros_like(total_ref)
        for at in range(0, channels + 4, 4):
            piece = point[at : at + 4] if at < channels else bias[:4]
            total_ref[:4, at // 4 * channels : (at // 4 + 1) * channels] = piece


def middle_call(rows_in, field, point, sat, readout, bias, inverse, back, lat_inv, lat_fwd, n):
    channels, rows = field.shape[:2]
    rr = 2 * rows
    per = KY * KZT // n
    whole = lambda a: pl.BlockSpec(a.shape, lambda y: (0,) * a.ndim)
    scalars = pl.BlockSpec(memory_space=pltpu.SMEM)
    return pl.pallas_call(
        partial(middle_kernel, n, rr),
        grid=(NY // YB,),
        out_shape=(
            jax.ShapeDtypeStruct(field.shape, BF),
            jax.ShapeDtypeStruct((n, channels * rr, per), BF),
            jax.ShapeDtypeStruct((8, LANES), F32),
        ),
        in_specs=[
            scalars, scalars,
            whole(rows_in),
            pl.BlockSpec((channels, rows, YB, NZT), lambda y: (0, 0, y, 0)),
            pl.BlockSpec((channels, rows, YB, NZT), lambda y: (0, 0, y, 0)),
            pl.BlockSpec((rows, YB, NZT), lambda y: (0, y, 0)),
            whole(inverse), whole(back),
            pl.BlockSpec((1,) + lat_inv.shape[1:], lambda y: (y, 0, 0)),
            pl.BlockSpec((1,) + lat_fwd.shape[1:], lambda y: (y, 0, 0)),
        ],
        out_specs=(
            pl.BlockSpec((channels, rows, YB, NZT), lambda y: (0, 0, y, 0)),
            pl.BlockSpec((n, channels * rr, per), lambda y: (0, 0, 0)),
            pl.BlockSpec((8, LANES), lambda y: (0, 0)),
        ),
        scratch_shapes=[
            pltpu.VMEM((channels // 2, KY * rr, 2 * LANES), F32),
            pltpu.VMEM((channels * rows * YB, 2 * LANES), BF),
            pltpu.VMEM((channels * 8 + 16, channels * 8), F32),
        ],
        compiler_params=params(58),
        name="middle",
    )(readout, bias, rows_in, field, point, sat, inverse, back, lat_inv, lat_fwd)


def last_kernel(
    rows_ref, grad_ref, table_ref, lat_inv_ref, spec_ref, back_ref, total_ref,
    out_ref, outer_ref, point_ref, bias_ref, flat,
):
    channels, rows = grad_ref.shape[:2]
    cells = rows * YB

    @pl.when(pl.program_id(0) == 0)
    def _():
        for at in range(0, channels, 4):
            point_ref[at : at + 4, :] = total_ref[:4, at // 4 * channels : (at // 4 + 1) * channels]
        bias_ref[...] = total_ref[:1, channels // 4 * channels : (channels // 4 + 1) * channels]

    planes(rows_ref, lat_inv_ref[0], flat, channels, cells)

    @pl.loop(0, channels // 4)
    def _(chunk):
        here = pl.ds(pl.multiple_of(chunk * 4 * cells, 4 * cells), 4 * cells)
        spectral = dot(flat[here, :], table_ref[...]).reshape(4, rows, YB, NZT)
        some = pl.ds(chunk * 4, 4)
        out_ref[some] = (spectral + grad_ref[some].astype(F32)).astype(BF)

    @pl.loop(0, outer_ref.shape[1])
    def _(i):
        s_real, s_imag = spec_ref[i, :KX], spec_ref[i, KX:]
        for o in range(channels):
            b_real, b_imag = back_ref[o, :KX], back_ref[o, KX:]
            outer_ref[0, i, o] = s_real * b_real + s_imag * b_imag
            outer_ref[1, i, o] = s_real * b_imag - s_imag * b_real


def last_call(rows_in, grad, table, lat_inv, spec, back_spec, total):
    channels, rows = grad.shape[:2]
    per = spec.shape[2]
    steps = NY // YB
    whole = lambda a: pl.BlockSpec(a.shape, lambda y: (0,) * a.ndim)
    block = pl.BlockSpec((channels, rows, YB, NZT), lambda y: (0, 0, y, 0))
    return pl.pallas_call(
        last_kernel,
        grid=(steps,),
        out_shape=(
            jax.ShapeDtypeStruct(grad.shape, BF),
            jax.ShapeDtypeStruct((2, channels, channels, KX, per), F32),
            jax.ShapeDtypeStruct((channels, channels), F32),
            jax.ShapeDtypeStruct((1, channels), F32),
        ),
        in_specs=[
            whole(rows_in), block, whole(table),
            pl.BlockSpec((1,) + lat_inv.shape[1:], lambda y: (y, 0, 0)),
            pl.BlockSpec((channels // steps,) + spec.shape[1:], lambda y: (y, 0, 0)),
            whole(back_spec), whole(total),
        ],
        out_specs=(
            block,
            pl.BlockSpec((2, channels // steps, channels, KX, per), lambda y: (0, y, 0, 0, 0)),
            pl.BlockSpec((channels, channels), lambda y: (0, 0)),
            pl.BlockSpec((1, channels), lambda y: (0, 0)),
        ),
        scratch_shapes=[
            pltpu.VMEM((channels * rows * YB, 2 * LANES), BF),
        ],
        compiler_params=params(58),
        name="last",
    )(rows_in, grad, table, lat_inv, spec, back_spec, total)


def local(n, lifted_field, saturation_grad, readout, spectral_weight, point_weight, point_bias):
    channels, rows = lifted_field.shape[:2]
    forward_table, inverse_table = plane_tables()
    lat_fwd, lat_inv, lat_whole = lateral_tables(rows)
    stream, stream_back = stream_tables(rows * n, rows)

    rows_in, spec, point_term = mix_call(
        spectral_weight, lifted_field, stream, stream_back, point_weight, n,
        tables=(narrow(forward_table), lat_whole),
    )
    grad_pre, sent_back, part = middle_call(
        rows_in, lifted_field, point_term, saturation_grad, readout, point_bias,
        narrow(inverse_table.T), narrow(inverse_table), lat_inv, lat_fwd, n,
    )
    rows_back, back_spec, point_in, total = mix_call(
        spectral_weight, grad_pre, stream, stream_back, point_weight, n, sent=sent_back, part=part
    )
    grad_field, grad_spectral, grad_point, grad_bias = last_call(
        rows_back, point_in, narrow(forward_table.T), lat_inv, spec, back_spec, total
    )
    return (grad_field, grad_spectral, grad_point, grad_bias.reshape(channels))


def solution(mesh):
    placed = (
        P(None, ("groups", "gx"), None, None),
        P(("groups", "gx"), None, None),
        P(),
        P(None, None, None, None, "gx"),
        P(),
        P(),
    )
    return jax.shard_map(
        partial(local, mesh.shape["gx"]),
        mesh=mesh,
        in_specs=placed,
        out_specs=(
            P(None, ("groups", "gx"), None, None),
            P("groups", None, None, None, "gx"),
            P("groups", None),
            P("groups"),
        ),
        check_vma=False,
    )
```

```python
from functools import partial
import math

import jax
import jax.numpy as jnp
import numpy as np
from jax import lax
from jax.experimental import pallas as pl
from jax.experimental.pallas import tpu as pltpu
from jax.sharding import PartitionSpec as P

NY = 128
NZ = 32
NT = 16
MX = 12
MY = 12
MZ = 6
MT = 4
NZT = 512
KZT = 48
KY = 2 * MY
KX = 2 * MX
LANES = 128
YB = 32
BF = jnp.bfloat16
F32 = jnp.float32
MESH = pl.DeviceIdType.MESH


def axis_tables(length, kept):
    positions = np.arange(length)
    frequency = np.concatenate([np.arange(kept), np.arange(length - kept, length)])
    angles = (frequency[:, None] * positions[None, :] % length) * (2.0 * math.pi / length)
    factor = 1.0 / math.sqrt(length)
    return np.cos(angles) * factor, np.sin(angles) * factor


def plane_tables():
    depth = np.concatenate([np.arange(MZ), np.arange(NZ - MZ, NZ)])
    phases = (
        depth[None, None, :, None] * np.arange(NZ)[:, None, None, None] * NT
        + np.arange(MT)[None, None, None, :] * np.arange(NT)[None, :, None, None] * NZ
    ) % NZT
    angles = phases * (2.0 * math.pi / NZT)
    factor = 1.0 / math.sqrt(NZT)
    cos_part = (np.cos(angles) * factor).reshape(NZT, KZT)
    sin_part = (np.sin(angles) * factor).reshape(NZT, KZT)
    weights = np.tile(np.where(np.arange(MT) == 0, 1.0, 2.0), 2 * MZ)
    forward = np.zeros((NZT, 2 * LANES))
    forward[:, :KZT], forward[:, LANES : LANES + KZT] = cos_part, -sin_part
    inverse = np.zeros((NZT, 2 * LANES))
    inverse[:, :KZT], inverse[:, LANES : LANES + KZT] = cos_part * weights, -sin_part * weights
    return forward, inverse


def narrow(table):
    return jnp.asarray(np.asarray(table, np.float32).astype(jnp.bfloat16))


def lateral_tables(rows):
    c, s = axis_tables(NY, MY)
    same = np.eye(rows)
    pairs = np.array([[c, s], [-s, c]])
    forward = np.einsum("rqky,xw->krxqwy", pairs, same)
    forward = forward.reshape(KY * 2 * rows, 2, rows, NY // YB, YB)
    forward = forward.transpose(3, 0, 1, 2, 4).reshape(NY // YB, KY * 2 * rows, 2 * rows * YB)
    inverse = np.einsum("rqky,xw->qwykrx", pairs, same)
    inverse = inverse.reshape(2, rows, NY // YB, YB, KY * 2 * rows)
    inverse = inverse.transpose(2, 0, 1, 3, 4).reshape(NY // YB, 2 * rows * YB, KY * 2 * rows)
    whole = np.einsum("rqky,xw->krxqwy", pairs, same).reshape(KY * 2 * rows, 2 * rows * NY)
    return narrow(forward), narrow(inverse), narrow(whole)


def stream_tables(cells, rows):
    c, s = axis_tables(cells, MX)
    pairs = np.array([[c, s], [-s, c]]).reshape(2, 2, KX, cells // rows, rows)
    table = np.einsum("rqkdx,ab->arkdbqx", pairs, np.eye(2))
    table = table.reshape(4 * KX, cells * 4)
    return narrow(table), narrow(table.T)


def mode_pieces(n):
    per = KY * KZT // n
    out = []
    for d in range(n):
        at, end, pieces = d * per, (d + 1) * per, []
        while at < end:
            ky, col = divmod(at, KZT)
            width = min(KZT - col, end - at)
            pieces.append((ky, col, width))
            at += width
        out.append(pieces)
    return out


def params(mib, **more):
    return pltpu.CompilerParams(vmem_limit_bytes=mib << 20, **more)


def dot(a, b):
    return jnp.dot(a, b, preferred_element_type=F32)


def pack(spectrum, out_ref, first_row, n, rr):
    for d, pieces in enumerate(mode_pieces(n)):
        halves = []
        for half in range(2):
            at = half * LANES
            parts = [
                spectrum[ky * rr : (ky + 1) * rr, at + col : at + col + width]
                for ky, col, width in pieces
            ]
            halves.append(jnp.concatenate(parts, axis=1))
        out_ref[d, pl.ds(first_row, 2 * rr), :] = jnp.concatenate(halves, axis=0).astype(BF)


def forward_kernel(n, rr, field_ref, plane_ref, lateral_ref, out_ref):
    cells = field_ref.shape[1] * NY
    flats = [
        dot(field_ref[half].reshape(cells, NZT), plane_ref[...]).astype(BF) for half in range(2)
    ]
    real = jnp.concatenate([f[:, :LANES] for f in flats], axis=1)
    imag = jnp.concatenate([f[:, LANES:] for f in flats], axis=1)
    spectrum = dot(lateral_ref[...], jnp.concatenate([real, imag], axis=0))
    pack(spectrum, out_ref, 0, n, rr)


def forward_part(n, rr, field_hbm, plane_ref, lateral_ref, sent, first, count):
    rows = field_hbm.shape[1]
    per = sent.shape[2]
    pltpu.emit_pipeline(
        lambda field_ref, out_ref: forward_kernel(
            n, rr, field_ref, plane_ref, lateral_ref, out_ref
        ),
        grid=(count,),
        in_specs=[pl.BlockSpec((2, rows, NY, NZT), lambda c: (c + first, 0, 0, 0))],
        out_specs=[pl.BlockSpec((n, 2 * rr, per), lambda c: (0, c + first, 0))],
    )(field_hbm, sent)


def exchange(n, source, target, send, recv, local, first, count):
    me, group = lax.axis_index("gx"), lax.axis_index("groups")
    rows = pl.ds(first, count)
    copies = []
    for k in range(1, n):
        peer = lax.rem(me + k, n)
        copy = pltpu.make_async_remote_copy(
            src_ref=source.at[peer, rows],
            dst_ref=target.at[me, rows],
            send_sem=send.at[k],
            recv_sem=recv.at[k],
            device_id=(group, peer),
            device_id_type=MESH,
        )
        copy.start()
        copies.append(copy)
    own = pltpu.make_async_copy(source.at[me, rows], target.at[me, rows], local)
    own.start()
    return copies + [own]


def spread_parts(n, source, target, send, recv, local):
    me, group = lax.axis_index("gx"), lax.axis_index("groups")
    copies = []
    for k in range(1, n):
        copy = pltpu.make_async_remote_copy(
            src_ref=source,
            dst_ref=target.at[me],
            send_sem=send.at[k],
            recv_sem=recv.at[k],
            device_id=(group, lax.rem(me + k, n)),
            device_id_type=MESH,
        )
        copy.start()
        copies.append(copy)
    own = pltpu.make_async_copy(source, target.at[me], local)
    own.start()
    return copies + [own]


def mix_kernel(n, rr, adjoint, weight_hbm, field_hbm, stream_ref, back_ref, point_ref, *refs):
    if adjoint:
        sent, part_ref, rows_out, spec_out, mixed_hbm, total_ref, *refs = refs
        *refs, parts, part_send, part_recv, part_local = refs
    else:
        plane_ref, lateral_ref, rows_out, spec_out, mixed_hbm, *refs = refs
        *refs, sent = refs
    got, weights, mixed_wire, got_back, kron, send, recv, local, weight_sem = refs
    rows = field_hbm.shape[1]
    channels = spec_out.shape[0]
    per = spec_out.shape[2]
    pairs = channels // 2
    early = pairs // 2
    me, group = lax.axis_index("gx"), lax.axis_index("groups")
    barrier = pltpu.get_barrier_semaphore()
    for k in range(1, n):
        pl.semaphore_signal(
            barrier, inc=1, device_id=(group, lax.rem(me + k, n)), device_id_type=MESH
        )
    fetch = pltpu.make_async_copy(weight_hbm, weights, weight_sem)
    fetch.start()

    def out(source, target, slot, first, count):
        return exchange(
            n, source, target, send.at[slot], recv.at[slot], local.at[slot],
            first * 2 * rr, count * 2 * rr,
        )

    if adjoint:
        pl.semaphore_wait(barrier, n - 1)
        copies = out(sent, got, 0, 0, pairs)
        shares = spread_parts(n, part_ref, parts, part_send, part_recv, part_local)
    else:
        forward_part(n, rr, field_hbm, plane_ref, lateral_ref, sent, 0, early)
        pl.semaphore_wait(barrier, n - 1)
        copies = out(sent, got, 0, 0, early)
        forward_part(n, rr, field_hbm, plane_ref, lateral_ref, sent, early, pairs - early)
        copies += out(sent, got, 1, early, pairs - early)
        shares = []
    point = point_ref[...] if adjoint else point_ref[...].astype(F32).T.astype(BF)
    kron[...] = kronecker(point, channels)
    pointwise(kron, field_hbm, mixed_hbm, 0, rows // 2)
    for copy in copies:
        copy.wait()

    @pl.loop(0, pairs)
    def _(pair):
        block = got[:, pl.ds(pl.multiple_of(pair * 2 * rr, 16), 2 * rr), :]
        both = dot(stream_ref[...], block.reshape(n * 2 * rr, per))
        spec_out[2 * pair] = both[: 2 * KX]
        spec_out[2 * pair + 1] = both[2 * KX :]

    fetch.wait()

    def mix(pair):
        results = []
        for half in range(2):
            o = 2 * pair + half
            real = jnp.zeros((KX, per), F32)
            imag = jnp.zeros((KX, per), F32)
            for i in range(channels):
                at = (o, i) if adjoint else (i, o)
                w_real = weights[0, at[0], at[1]].astype(F32)
                w_imag = weights[1, at[0], at[1]].astype(F32)
                s_real = spec_out[i, :KX]
                s_imag = spec_out[i, KX:]
                if adjoint:
                    real += w_real * s_real + w_imag * s_imag
                    imag += w_real * s_imag - w_imag * s_real
                else:
                    real += w_real * s_real - w_imag * s_imag
                    imag += w_real * s_imag + w_imag * s_real
            results += [real, imag]
        both = dot(back_ref[...], jnp.concatenate(results, axis=0).astype(BF)).astype(BF)
        mixed_wire[:, pl.ds(pl.multiple_of(pair * 2 * rr, 16), 2 * rr), :] = both.reshape(
            n, 2 * rr, per
        )

    pl.loop(0, early)(mix)
    copies = out(mixed_wire, got_back, 2, 0, early)
    pl.loop(early, pairs)(mix)
    copies += out(mixed_wire, got_back, 3, early, pairs - early)
    pointwise(kron, field_hbm, mixed_hbm, rows // 2, rows - rows // 2)
    for copy in copies + shares:
        copy.wait()
    if adjoint:
        total = parts[0]
        for d in range(1, n):
            total = total + parts[d]
        total_ref[...] = total

    pieces_of = mode_pieces(n)

    @pl.loop(0, channels // 2)
    def _(pair):
        found = [[[] for _ in range(KY)] for _ in range(2)]
        for d in range(n):
            block = got_back[d, pl.ds(pl.multiple_of(pair * 2 * rr, 16), 2 * rr), :].astype(F32)
            at = 0
            for ky, _, width in pieces_of[d]:
                for half in range(2):
                    found[half][ky].append(block[half * rr : (half + 1) * rr, at : at + width])
                at += width
        lanes = jnp.zeros((rr, LANES - KZT), F32)
        halves = [
            jnp.concatenate(
                [jnp.concatenate(found[half][ky] + [lanes], axis=1) for ky in range(KY)], axis=0
            )
            for half in range(2)
        ]
        rows_out[pair] = jnp.concatenate(halves, axis=1).astype(BF)


def mix_call(weight, field, stream, stream_back, point, n, sent=None, part=None, tables=None):
    channels, rows = field.shape[:2]
    rr = 2 * rows
    per = weight.shape[4]
    adjoint = sent is not None
    wire = (n, channels * rr, per)
    vmem = pl.BlockSpec(memory_space=pltpu.VMEM)
    hbm = pl.BlockSpec(memory_space=pl.ANY)
    out_shape = [
        jax.ShapeDtypeStruct((channels // 2, KY * rr, 2 * LANES), BF),
        jax.ShapeDtypeStruct((channels, 2 * KX, per), F32),
        jax.ShapeDtypeStruct(field.shape, BF),
    ]
    scratch = [
        pltpu.VMEM(wire, BF),
        pltpu.VMEM(weight.shape, BF),
        pltpu.VMEM(wire, BF),
        pltpu.VMEM(wire, BF),
        pltpu.VMEM((channels * 8, channels * 8), BF),
        pltpu.SemaphoreType.DMA((4, n)),
        pltpu.SemaphoreType.DMA((4, n)),
        pltpu.SemaphoreType.DMA((4,)),
        pltpu.SemaphoreType.DMA(()),
    ]
    operands = [weight, field, stream, stream_back, point]
    if adjoint:
        out_shape.append(jax.ShapeDtypeStruct(part.shape, F32))
        scratch += [
            pltpu.VMEM((n,) + part.shape, F32),
            pltpu.SemaphoreType.DMA((n,)),
            pltpu.SemaphoreType.DMA((n,)),
            pltpu.SemaphoreType.DMA(()),
        ]
        operands += [sent, part]
    else:
        scratch.append(pltpu.VMEM(wire, BF))
        operands += list(tables)
    return pl.pallas_call(
        partial(mix_kernel, n, rr, adjoint),
        out_shape=out_shape,
        in_specs=[hbm, hbm] + [vmem] * (len(operands) - 2),
        out_specs=[vmem, vmem, hbm] + [vmem] * (len(out_shape) - 3),
        scratch_shapes=scratch,
        compiler_params=params(58, collective_id=int(adjoint), has_side_effects=True),
        name="adjoint_mix" if adjoint else "forward_mix",
    )(*operands)


def gelu_slope(v):
    cumulative = 0.5 + 0.5 * lax.erf(v * 0.7071067811865476)
    return cumulative + v * (jnp.exp(-0.5 * v * v) * 0.3989422804014327)


def planes(rows_ref, lateral, flat, channels, cells):
    @pl.loop(0, channels // 2, unroll=5)
    def _(pair):
        both = dot(lateral, rows_ref[pair]).astype(BF)
        for half in range(2):
            at = slice(half * LANES, (half + 1) * LANES)
            plane = jnp.concatenate([both[:cells, at], both[cells:, at]], axis=1)
            flat[pl.ds(pl.multiple_of((2 * pair + half) * cells, cells), cells), :] = plane


def pointwise(kron, source, target, first, count):
    channels = source.shape[0]

    def body(block_ref, out_ref):
        for yb in range(YB // 8):
            y8 = slice(yb * 8, yb * 8 + 8)
            block = block_ref[:, 0, y8, :].reshape(channels * 8, NZT)
            out_ref[:, 0, y8, :] = dot(kron[...], block).astype(BF).reshape(channels, 8, NZT)

    spec = pl.BlockSpec((channels, 1, YB, NZT), lambda x, y: (0, first + x, y, 0))
    pltpu.emit_pipeline(body, grid=(count, NY // YB), in_specs=[spec], out_specs=[spec])(
        source, target
    )


def expand(channels):
    row = lax.broadcasted_iota(jnp.int32, (channels * 8, channels), 0)
    column = lax.broadcasted_iota(jnp.int32, (channels * 8, channels), 1)
    spread = ((row >= column * 8) & (row < column * 8 + 8)).astype(BF)
    wide = (channels * 8, channels * 8)
    phase = lax.broadcasted_iota(jnp.int32, wide, 0) - lax.broadcasted_iota(jnp.int32, wide, 1)
    return spread, lax.rem(phase + channels * 8, 8) == 0


def kronecker(weight, channels):
    spread, mask = expand(channels)
    wide = lax.dot_general(
        dot(spread, weight).astype(BF), spread, (((1,), (1,)), ((), ())), preferred_element_type=F32
    )
    return jnp.where(mask, wide, 0.0).astype(BF)


def middle_kernel(
    n, rr, readout_ref, bias_ref, rows_ref, field_ref, point_ref, sat_ref, inverse_ref, back_ref,
    lat_inv_ref, lat_fwd_ref, grad_ref, wire_ref, total_ref, spectrum, flat, corr,
):
    step = pl.program_id(0)
    channels, rows = field_ref.shape[:2]
    cells = rows * YB

    @pl.when(step == 0)
    def _():
        corr[...] = jnp.zeros_like(corr)
        spectrum[...] = jnp.zeros_like(spectrum)

    planes(rows_ref, lat_inv_ref[0], flat, channels, cells)

    @pl.loop(0, channels // 2, unroll=5)
    def _(pair):
        here = pl.ds(pl.multiple_of(pair * 2 * cells, 2 * cells), 2 * cells)
        both = dot(flat[here, :], inverse_ref[...])
        sat = sat_ref[...].reshape(cells, NZT).astype(F32)
        for half in range(2):
            o = 2 * pair + half
            pre = both[half * cells : (half + 1) * cells]
            pre = pre + point_ref[o].reshape(cells, NZT).astype(F32) + bias_ref[o]
            grad = (readout_ref[o] * sat * gelu_slope(pre)).astype(BF)
            grad_ref[o] = grad.reshape(rows, YB, NZT)

    @pl.loop(0, rows, unroll=True)
    def _(x):
        lefts, rights = [], []
        for yb in range(YB // 8):
            y8 = slice(yb * 8, yb * 8 + 8)
            block = field_ref[:, x, y8, :].reshape(channels * 8, NZT)
            lefts.append(jnp.concatenate([block, jnp.ones((16, NZT), BF)], axis=0))
            rights.append(grad_ref[:, x, y8, :].reshape(channels * 8, NZT))
        corr[...] += lax.dot_general(
            jnp.concatenate(lefts, axis=1),
            jnp.concatenate(rights, axis=1),
            (((1,), (1,)), ((), ())),
            preferred_element_type=F32,
        )

    some = 4 * cells

    @pl.loop(0, channels // 4)
    def _(chunk):
        grads = grad_ref[pl.ds(chunk * 4, 4)].reshape(some, NZT)
        flat[pl.ds(pl.multiple_of(chunk * some, some), some), :] = dot(grads, back_ref[...]).astype(BF)

    @pl.loop(0, channels // 2, unroll=5)
    def _(pair):
        flats = [
            flat[pl.ds(pl.multiple_of((2 * pair + half) * cells, cells), cells), :]
            for half in range(2)
        ]
        real = jnp.concatenate([f[:, :LANES] for f in flats], axis=1)
        imag = jnp.concatenate([f[:, LANES:] for f in flats], axis=1)
        spectrum[pair] += dot(lat_fwd_ref[0], jnp.concatenate([real, imag], axis=0))

    @pl.when(step == pl.num_programs(0) - 1)
    def _():
        @pl.loop(0, channels // 2)
        def _(pair):
            pack(spectrum[pair], wire_ref, pl.multiple_of(pair * 2 * rr, 16), n, rr)

        spread, mask = expand(channels)
        spread = spread.astype(F32)
        best = partial(
            lax.dot_general, preferred_element_type=F32, precision=lax.Precision.HIGHEST
        )
        sums = jnp.where(mask, corr[: channels * 8], 0.0)
        inner = best(sums, spread, (((1,), (0,)), ((), ())))
        point = best(spread, inner, (((0,), (0,)), ((), ())))
        bias = best(corr[channels * 8 : channels * 8 + 8], spread, (((1,), (0,)), ((), ())))
        total_ref[...] = jnp.zeros_like(total_ref)
        for at in range(0, channels + 4, 4):
            piece = point[at : at + 4] if at < channels else bias[:4]
            total_ref[:4, at // 4 * channels : (at // 4 + 1) * channels] = piece


def middle_call(rows_in, field, point, sat, readout, bias, inverse, back, lat_inv, lat_fwd, n):
    channels, rows = field.shape[:2]
    rr = 2 * rows
    per = KY * KZT // n
    whole = lambda a: pl.BlockSpec(a.shape, lambda y: (0,) * a.ndim)
    scalars = pl.BlockSpec(memory_space=pltpu.SMEM)
    return pl.pallas_call(
        partial(middle_kernel, n, rr),
        grid=(NY // YB,),
        out_shape=(
            jax.ShapeDtypeStruct(field.shape, BF),
            jax.ShapeDtypeStruct((n, channels * rr, per), BF),
            jax.ShapeDtypeStruct((8, LANES), F32),
        ),
        in_specs=[
            scalars, scalars,
            whole(rows_in),
            pl.BlockSpec((channels, rows, YB, NZT), lambda y: (0, 0, y, 0)),
            pl.BlockSpec((channels, rows, YB, NZT), lambda y: (0, 0, y, 0)),
            pl.BlockSpec((rows, YB, NZT), lambda y: (0, y, 0)),
            whole(inverse), whole(back),
            pl.BlockSpec((1,) + lat_inv.shape[1:], lambda y: (y, 0, 0)),
            pl.BlockSpec((1,) + lat_fwd.shape[1:], lambda y: (y, 0, 0)),
        ],
        out_specs=(
            pl.BlockSpec((channels, rows, YB, NZT), lambda y: (0, 0, y, 0)),
            pl.BlockSpec((n, channels * rr, per), lambda y: (0, 0, 0)),
            pl.BlockSpec((8, LANES), lambda y: (0, 0)),
        ),
        scratch_shapes=[
            pltpu.VMEM((channels // 2, KY * rr, 2 * LANES), F32),
            pltpu.VMEM((channels * rows * YB, 2 * LANES), BF),
            pltpu.VMEM((channels * 8 + 16, channels * 8), F32),
        ],
        compiler_params=params(58),
        name="middle",
    )(readout, bias, rows_in, field, point, sat, inverse, back, lat_inv, lat_fwd)


def last_kernel(
    rows_ref, grad_ref, table_ref, lat_inv_ref, spec_ref, back_ref, total_ref,
    out_ref, outer_ref, point_ref, bias_ref, flat,
):
    channels, rows = grad_ref.shape[:2]
    cells = rows * YB

    @pl.when(pl.program_id(0) == 0)
    def _():
        for at in range(0, channels, 4):
            point_ref[at : at + 4, :] = total_ref[:4, at // 4 * channels : (at // 4 + 1) * channels]
        bias_ref[...] = total_ref[:1, channels // 4 * channels : (channels // 4 + 1) * channels]

    planes(rows_ref, lat_inv_ref[0], flat, channels, cells)

    @pl.loop(0, channels // 4, unroll=5)
    def _(chunk):
        here = pl.ds(pl.multiple_of(chunk * 4 * cells, 4 * cells), 4 * cells)
        spectral = dot(flat[here, :], table_ref[...]).reshape(4, rows, YB, NZT)
        some = pl.ds(chunk * 4, 4)
        out_ref[some] = (spectral + grad_ref[some].astype(F32)).astype(BF)

    @pl.loop(0, outer_ref.shape[1])
    def _(i):
        s_real, s_imag = spec_ref[i, :KX], spec_ref[i, KX:]
        for o in range(channels):
            b_real, b_imag = back_ref[o, :KX], back_ref[o, KX:]
            outer_ref[0, i, o] = s_real * b_real + s_imag * b_imag
            outer_ref[1, i, o] = s_real * b_imag - s_imag * b_real


def last_call(rows_in, grad, table, lat_inv, spec, back_spec, total):
    channels, rows = grad.shape[:2]
    per = spec.shape[2]
    steps = NY // YB
    whole = lambda a: pl.BlockSpec(a.shape, lambda y: (0,) * a.ndim)
    block = pl.BlockSpec((channels, rows, YB, NZT), lambda y: (0, 0, y, 0))
    return pl.pallas_call(
        last_kernel,
        grid=(steps,),
        out_shape=(
            jax.ShapeDtypeStruct(grad.shape, BF),
            jax.ShapeDtypeStruct((2, channels, channels, KX, per), F32),
            jax.ShapeDtypeStruct((channels, channels), F32),
            jax.ShapeDtypeStruct((1, channels), F32),
        ),
        in_specs=[
            whole(rows_in), block, whole(table),
            pl.BlockSpec((1,) + lat_inv.shape[1:], lambda y: (y, 0, 0)),
            pl.BlockSpec((channels // steps,) + spec.shape[1:], lambda y: (y, 0, 0)),
            whole(back_spec), whole(total),
        ],
        out_specs=(
            block,
            pl.BlockSpec((2, channels // steps, channels, KX, per), lambda y: (0, y, 0, 0, 0)),
            pl.BlockSpec((channels, channels), lambda y: (0, 0)),
            pl.BlockSpec((1, channels), lambda y: (0, 0)),
        ),
        scratch_shapes=[
            pltpu.VMEM((channels * rows * YB, 2 * LANES), BF),
        ],
        compiler_params=params(58),
        name="last",
    )(rows_in, grad, table, lat_inv, spec, back_spec, total)


def local(n, lifted_field, saturation_grad, readout, spectral_weight, point_weight, point_bias):
    channels, rows = lifted_field.shape[:2]
    forward_table, inverse_table = plane_tables()
    lat_fwd, lat_inv, lat_whole = lateral_tables(rows)
    stream, stream_back = stream_tables(rows * n, rows)

    rows_in, spec, point_term = mix_call(
        spectral_weight, lifted_field, stream, stream_back, point_weight, n,
        tables=(narrow(forward_table), lat_whole),
    )
    grad_pre, sent_back, part = middle_call(
        rows_in, lifted_field, point_term, saturation_grad, readout, point_bias,
        narrow(inverse_table.T), narrow(inverse_table), lat_inv, lat_fwd, n,
    )
    rows_back, back_spec, point_in, total = mix_call(
        spectral_weight, grad_pre, stream, stream_back, point_weight, n, sent=sent_back, part=part
    )
    grad_field, grad_spectral, grad_point, grad_bias = last_call(
        rows_back, point_in, narrow(forward_table.T), lat_inv, spec, back_spec, total
    )
    return (grad_field, grad_spectral, grad_point, grad_bias.reshape(channels))


def solution(mesh):
    placed = (
        P(None, ("groups", "gx"), None, None),
        P(("groups", "gx"), None, None),
        P(),
        P(None, None, None, None, "gx"),
        P(),
        P(),
    )
    return jax.shard_map(
        partial(local, mesh.shape["gx"]),
        mesh=mesh,
        in_specs=placed,
        out_specs=(
            P(None, ("groups", "gx"), None, None),
            P("groups", None, None, None, "gx"),
            P("groups", None),
            P("groups"),
        ),
        check_vma=False,
    )
```
